32 devices in a mesh: cube: 32 (over z, y, x, core).
Axes of the slice: x: 2, y: 2, z: 4, core: 2. Of those that a mesh axis runs over, the one named last changes fastest.
Arguments:
- offsets: float32 [3, 131072], P(None, 'cube'), may hold values from 0 to 1
- charges: float32 [16, 131072], P(None, 'cube'), may hold values from -6 to 6
- counts: int32 [1024], P('cube'), may hold values from 1 to 128, as said below
- u_list: int32 [1024, 27], P('cube'), may hold values from 0 to 1023, as said below
- v_src: int32 [1024, 32], P('cube'), may hold values from 0 to 111, as said below
- v_type: int32 [1024, 32], P('cube'), may hold values from 0 to 15
- wanted: int32 [32, 5, 16], P('cube'), may hold values from 0 to 31, as said below
- m2l: float32 [152, 2432], replicated, may hold values from -0.078125 to 0.078125
- uc2e: float32 [152, 152], replicated, may hold values from -0.5 to 0.5
- dc2e: float32 [152, 152], replicated, may hold values from -0.5 to 0.5
Outputs:
- potential: float32 [16, 131072], P(None, 'cube')
The draws below stay inside these ranges and needn't reach their ends.
Inputs may be any that keep to these rules, and one draw needn't show every extreme that they name: `counts`: every leaf has at least one live point; the first leaf of each device is full. `u_list`: entry 0 of each row is the leaf itself; every entry lies within 8 leaves of the leaf in the global order. `v_src`: codes below 80 name hypercube dimension v // 16 and reader slot v % 16; larger codes name a leaf of the same device; entry 0 of each row is the leaf itself. `wanted`: entries of one list are distinct local leaf indices of the partner.
All inputs are finite; a program needn't handle non-finite values.
Results may differ from the reference program's by a relative error of at most 0.0003.
Values sent between devices are 32-bit elements; how exact they have to be, the bound alone decides.
No kernel may reach another device: no remote copies, remote signals or barrier semaphores. Data moves between devices by JAX's collectives and lax.ppermute only.
A program may use at most 64 MiB of HBM per device.

```python
import math
import jax
import jax.numpy as jnp
import numpy as np
from jax import lax

LEAVES_DEV = 32
LEAF_PTS = 128
PROBES = 16
EQUIV = 152
TYPES = 16
U_SLOTS = 27
V_SLOTS = 32
GHOST = 8
READ_CAP = 16
DEVICE_COUNT = 32
BITS = 5
LEAVES = 1024
POINTS = 131072
N_CUBE = 32


def draw_counts(key, part):
    drawn = jax.random.randint(key, (LEAVES,), 1, LEAF_PTS + 1)
    leading = jnp.arange(LEAVES, dtype=jnp.int32) % LEAVES_DEV == 0
    return jnp.where(leading, LEAF_PTS, drawn).astype(jnp.int32)


def draw_u_list(key, part):
    leaf_ids = jnp.arange(LEAVES, dtype=jnp.int32)[:, None]
    moved = jax.random.randint(key, (LEAVES, U_SLOTS), -GHOST, GHOST + 1)
    moved = moved.at[:, 0].set(0)
    return jnp.clip(leaf_ids + moved, 0, LEAVES - 1).astype(jnp.int32)


def draw_v_src(key, part):
    first_key, second_key, third_key = jax.random.split(key, 3)
    chosen_bit = jax.random.randint(first_key, (LEAVES, V_SLOTS), 0, BITS + 1)
    remote = chosen_bit * READ_CAP + jax.random.randint(second_key, (LEAVES, V_SLOTS), 0, READ_CAP)
    own_leaf = BITS * READ_CAP + jax.random.randint(third_key, (LEAVES, V_SLOTS), 0, LEAVES_DEV)
    values = jnp.where(chosen_bit < BITS, remote, own_leaf)
    itself = BITS * READ_CAP + jnp.arange(LEAVES, dtype=jnp.int32) % LEAVES_DEV
    values = values.at[:, 0].set(itself)
    return values.astype(jnp.int32)


def draw_wanted(key, part):
    scores = jax.random.randint(key, (DEVICE_COUNT, BITS, LEAVES_DEV), 0, 1 << 20)
    scores = scores * LEAVES_DEV + jnp.arange(LEAVES_DEV, dtype=jnp.int32)
    ranked = jnp.argsort(scores, axis=-1)
    return ranked[:, :, :READ_CAP].astype(jnp.int32)


def plant(values, rng, low, top_value):
    index_at = [jax.random.randint(jax.random.fold_in(rng, axis), (), 0, length) for axis, length in enumerate(values.shape)]
    widest = values.shape.index(max(values.shape))
    neighbour = index_at[:widest] + [(index_at[widest] + 1) % values.shape[widest]] + index_at[widest + 1:]
    return values.at[tuple(index_at)].set(low).at[tuple(neighbour)].set(top_value)


def block_scale(key, dims, cuts, smallest, largest):
    factor_of = 1.0
    for dim, blocks in cuts:
        steps = jax.random.uniform(jax.random.fold_in(jax.random.fold_in(key, 6), dim), (blocks,), jnp.float32, smallest / len(cuts), largest / len(cuts))
        factor_of = factor_of * jnp.repeat(jnp.exp(steps), dims[dim] // blocks).reshape((-1,) + (1,) * (len(dims) - 1 - dim))
    return factor_of


def bell_draw(stream_key, shape, deviation, limit, cuts=(), kind=jnp.bfloat16):
    values = deviation * jax.random.normal(stream_key, shape, jnp.float32)
    if cuts:
        values = values * block_scale(stream_key, shape, cuts, -0.22, 0.18)
    return jnp.clip(values, -limit, limit).astype(kind)


def setup_inputs(seed: int = 0) -> dict:
    key_of = jax.random.split(jax.random.key(seed), 11)
    return {
        "offsets": jnp.clip(1.0 * jax.random.uniform(key_of[0], (3, POINTS), jnp.float32) ** block_scale(key_of[0], (3, POINTS), ((1, 32),), -0.2, 0.2), 0.0, 1.0),
        "charges": bell_draw(key_of[1], (PROBES, POINTS), 1.0, 6.0, ((1, 32),), jnp.float32),
        "counts": draw_counts(jax.random.fold_in(key_of[10], 71), 0),
        "u_list": draw_u_list(jax.random.fold_in(key_of[10], 71), 0),
        "v_src": draw_v_src(jax.random.fold_in(key_of[10], 71), 0),
        "v_type": plant(jax.random.randint(key_of[5], (LEAVES, V_SLOTS), 0, TYPES), jax.random.fold_in(key_of[5], 1), 0, TYPES - 1).astype(jnp.int32),
        "wanted": draw_wanted(jax.random.fold_in(key_of[10], 71), 0),
        "m2l": bell_draw(key_of[7], (EQUIV, TYPES * EQUIV), (V_SLOTS * EQUIV) ** -0.5, 0.078125, (), jnp.float32),
        "uc2e": bell_draw(key_of[8], (EQUIV, EQUIV), EQUIV ** -0.5, 0.5, (), jnp.float32),
        "dc2e": bell_draw(key_of[9], (EQUIV, EQUIV), EQUIV ** -0.5, 0.5, (), jnp.float32),
    }


soften = 0.01
inv_four_pi = 1.0 / (4.0 * math.pi)
surface_radius = 0.55
highest = lax.Precision.HIGHEST

def surface_table():
    lattice = np.arange(6)
    coords = np.stack(np.meshgrid(lattice, lattice, lattice, indexing='ij'), 0).reshape(3, -1)
    coords = (coords - 2.5) / 2.5
    on_face = np.max(np.abs(coords), axis=0) > 0.99
    return coords[:, on_face].astype(np.float32)

def leaf_corner(leaf_ids):
    corners = []
    for axis_num in range(3):
        summed = jnp.zeros_like(leaf_ids)
        for digit_num in range(10):
            summed = summed + ((leaf_ids >> 3 * digit_num + axis_num & 1) << digit_num)
        corners.append(summed)
    return jnp.stack(corners, 0).astype(jnp.float32)

def kernel(targets, sources):
    squared = jnp.zeros((targets.shape[-1], sources.shape[-1]), jnp.float32)
    for axis_num in range(3):
        squared = squared + (targets[axis_num][:, None] - sources[axis_num][None, :]) ** 2
    return inv_four_pi * lax.rsqrt(squared + soften)

def upward(points, masked, centers, surface, uc2e):
    checks = centers[:, :, None] + surface_radius * surface[:, None, :]
    tiles = jax.vmap(kernel, in_axes=(1, 1))(checks, points)
    potent = jnp.einsum('ljp,qlp->lqj', tiles, masked, precision=highest)
    return jnp.einsum('lqj,ij->lqi', potent, uc2e, precision=highest)

def downward(points, centers, surface, downcheck, dc2e):
    downeq = jnp.einsum('lqi,ji->lqj', downcheck, dc2e, precision=highest)
    equivs = centers[:, :, None] + surface_radius * surface[:, None, :]
    tiles = jax.vmap(kernel, in_axes=(1, 1))(points, equivs)
    return jnp.einsum('lpj,lqj->qlp', tiles, downeq, precision=highest)

def near_field(targets, src_pts, src_chg):
    leaf_count = targets.shape[0]
    group = math.gcd(leaf_count, 8)
    blocks = leaf_count // group

    def one_group(packed):
        tgt, spt, sch = packed
        tiles = jax.vmap(kernel)(tgt, spt)
        return jnp.einsum('gpn,gqn->gqp', tiles, sch, precision=highest)
    result = lax.map(one_group, (targets.reshape(blocks, group, targets.shape[1], targets.shape[2]), src_pts.reshape(blocks, group, src_pts.shape[1], src_pts.shape[2]), src_chg.reshape(blocks, group, src_chg.shape[1], src_chg.shape[2])))
    return result.reshape(leaf_count, src_chg.shape[1], targets.shape[2])

def reference(offsets, charges, counts, u_list, v_src, v_type, wanted, m2l, uc2e, dc2e):
    total = counts.shape[0]
    surface = jnp.asarray(surface_table())
    m2l_ops = m2l.reshape(EQUIV, TYPES, EQUIV)
    inside = (jnp.arange(LEAF_PTS, dtype=jnp.int32)[None, :] < counts[:, None]).astype(jnp.float32)
    leaf_ids = jnp.arange(total, dtype=jnp.int32)
    corners = leaf_corner(leaf_ids)
    centers = corners + 0.5
    points = offsets.reshape(3, total, LEAF_PTS) + corners[:, :, None]
    masked = charges.reshape(PROBES, total, LEAF_PTS) * inside[None]

    def up_device(device):
        start = (device * LEAVES_DEV).astype(jnp.int32)
        pts = lax.dynamic_slice_in_dim(points, start, LEAVES_DEV, 1)
        chg = lax.dynamic_slice_in_dim(masked, start, LEAVES_DEV, 1)
        ctr = lax.dynamic_slice_in_dim(centers, start, LEAVES_DEV, 1)
        return upward(pts, chg, ctr, surface, uc2e)
    devices = jnp.arange(N_CUBE, dtype=jnp.int32)
    up_all = lax.map(up_device, devices).reshape(total, PROBES, EQUIV)
    onehot_types = jnp.arange(TYPES, dtype=jnp.int32)

    def out_device(device):
        start = (device * LEAVES_DEV).astype(jnp.int32)
        pts = lax.dynamic_slice_in_dim(points, start, LEAVES_DEV, 1)
        ctr = lax.dynamic_slice_in_dim(centers, start, LEAVES_DEV, 1)
        live = lax.dynamic_slice_in_dim(inside, start, LEAVES_DEV, 0)
        codes = lax.dynamic_slice_in_dim(v_src, start, LEAVES_DEV, 0)
        kinds = lax.dynamic_slice_in_dim(v_type, start, LEAVES_DEV, 0)
        near_ids = lax.dynamic_slice_in_dim(u_list, start, LEAVES_DEV, 0)
        bit_part = jnp.minimum(codes // READ_CAP, BITS - 1)
        slot_part = codes % READ_CAP
        remote_leaf = wanted[device][bit_part, slot_part]
        partner = jnp.bitwise_xor(device, jnp.left_shift(jnp.int32(1), bit_part))
        sources = jnp.where(codes >= BITS * READ_CAP, start + codes - BITS * READ_CAP, partner * LEAVES_DEV + remote_leaf).astype(jnp.int32)
        gathered = up_all[sources]
        onehot = (kinds[:, :, None] == onehot_types[None, None, :]).astype(jnp.float32)
        by_type = jnp.einsum('lvt,lvqj->ltqj', onehot, gathered, precision=highest)
        downcheck = jnp.einsum('ltqj,itj->lqi', by_type, m2l_ops, precision=highest)
        far = downward(pts, ctr, surface, downcheck, dc2e)
        src_pts = points[:, near_ids].transpose(1, 0, 2, 3).reshape(LEAVES_DEV, 3, U_SLOTS * LEAF_PTS)
        src_chg = masked[:, near_ids].transpose(1, 0, 2, 3).reshape(LEAVES_DEV, PROBES, U_SLOTS * LEAF_PTS)
        near = near_field(pts.transpose(1, 0, 2), src_pts, src_chg).transpose(1, 0, 2)
        return (near + far) * live[None]
    result = lax.map(out_device, devices)
    return result.transpose(1, 0, 2, 3).reshape(PROBES, total * LEAF_PTS)
```

```python
import math

import jax
import jax.numpy as jnp
import numpy as np
from jax import lax
from jax.experimental import pallas as pl
from jax.experimental.pallas import tpu as pltpu
from jax.sharding import PartitionSpec as P

GHOST = 8
PTS = 128


soften = 0.01
inv_four_pi = 1.0 / (4.0 * math.pi)
surface_radius = 0.55
highest = lax.Precision.HIGHEST


def halo(block, axis, width):
    count = lax.axis_size(axis)
    forward = [(i, i + 1) for i in range(count - 1)]
    backward = [(target, source) for source, target in forward]
    low = lax.ppermute(block[:, block.shape[1] - width:], axis, forward)
    high = lax.ppermute(block[:, :width], axis, backward)
    return low, high


def from_partner(array, axis, bit):
    return lax.ppermute(array, axis, [(i, i ^ 1 << bit) for i in range(lax.axis_size(axis))])


def surface_table():
    lattice = np.arange(6)
    coords = np.stack(np.meshgrid(lattice, lattice, lattice, indexing="ij"), 0).reshape(3, -1)
    coords = (coords - 2.5) / 2.5
    on_face = np.max(np.abs(coords), axis=0) > 0.99
    return coords[:, on_face].astype(np.float32)


def leaf_corner(leaf_ids):
    corners = []
    for axis_num in range(3):
        summed = jnp.zeros_like(leaf_ids)
        for digit_num in range(10):
            summed = summed + ((leaf_ids >> 3 * digit_num + axis_num & 1) << digit_num)
        corners.append(summed)
    return jnp.stack(corners, 0).astype(jnp.float32)


def kernel(targets, sources):
    squared = jnp.zeros((targets.shape[-1], sources.shape[-1]), jnp.float32)
    for axis_num in range(3):
        squared = squared + (targets[axis_num][:, None] - sources[axis_num][None, :]) ** 2
    return inv_four_pi * lax.rsqrt(squared + soften)


def upward(points, masked, centers, surface, uc2e):
    checks = centers[:, :, None] + surface_radius * surface[:, None, :]
    tiles = jax.vmap(kernel, in_axes=(1, 1))(checks, points)
    potent = jnp.einsum("ljp,qlp->lqj", tiles, masked, precision=highest)
    return jnp.einsum("lqj,ij->lqi", potent, uc2e, precision=highest)


def downward(points, centers, surface, downcheck, dc2e):
    downeq = jnp.einsum("lqi,ji->lqj", downcheck, dc2e, precision=highest)
    equivs = centers[:, :, None] + surface_radius * surface[:, None, :]
    tiles = jax.vmap(kernel, in_axes=(1, 1))(points, equivs)
    return jnp.einsum("lpj,lqj->qlp", tiles, downeq, precision=highest)


def near_kernel(first_ref, counts_ref, own_ref, low_ref, high_ref, ulist_ref, out_ref,
                lanes_ref, chg_ref, src_ref, mult_ref, res_ref, start_ref, leaf_ref, from_ref, to_ref):
    f32, bf16, i32 = jnp.float32, jnp.bfloat16, jnp.int32
    local = out_ref.shape[1] // PTS
    every = local + 2 * GHOST
    probes = out_ref.shape[0]
    base = GHOST * PTS
    lane = lax.broadcasted_iota(i32, (1, PTS), 1)

    first = first_ref[0]
    centre = []
    for axis in range(3):
        low = high = jnp.int32(0)
        for digit in range(10):
            low = low + (((first >> (3 * digit + axis)) & 1) << digit)
            high = high + ((((first + local - 1) >> (3 * digit + axis)) & 1) << digit)
        centre.append((low + high + 1).astype(f32) * 0.5)
    sub = lax.broadcasted_iota(i32, (8, PTS), 0)
    shift_by = jnp.where(sub == 0, centre[0], jnp.where(sub == 1, centre[1], jnp.where(sub == 2, centre[2], 0.0)))

    def units(n):
        return ((n + 15) // 16) * 16

    def ghost_count(ref, e):
        return jnp.max(ref[3:4, e * PTS:(e + 1) * PTS]).astype(i32)

    starts = [None] * (every + 1)
    starts[GHOST] = jnp.int32(base)
    for e in range(GHOST - 1, -1, -1):
        starts[e] = starts[e + 1] - units(ghost_count(low_ref, e))
    for e in range(GHOST, GHOST + local):
        starts[e + 1] = starts[e] + units(counts_ref[e - GHOST])
    for e in range(GHOST + local, every):
        starts[e + 1] = starts[e] + units(ghost_count(high_ref, e - GHOST - local))
    for e in range(every + 1):
        start_ref[e] = starts[e]

    for i in range(8):
        leaf_ref[jnp.maximum((starts[0] >> 4) - 8 + i, 0)] = 0
    for e in range(every):
        for i in range(8 if e < every - 1 else 48):
            leaf_ref[(starts[e] >> 4) + i] = e

    for e in range(GHOST, GHOST + local):
        head = starts[e] - base
        tail = starts[e + 1] - base - 1
        @pl.when(tail >= head)
        def _():
            h, t = head >> 8, tail >> 8

            @pl.when((head & 255) == 0)
            def _():
                from_ref[h] = e

            @pl.when(t > h)
            def _():
                from_ref[t] = e

            to_ref[h] = e
            to_ref[t] = e

    ids = ulist_ref[...] - (first - GHOST)
    which = lax.broadcasted_iota(i32, (local, every), 1)
    tally = jnp.zeros((local, every), f32)
    for u in range(ids.shape[1]):
        tally = tally + (ids[:, u:u + 1] == which).astype(f32)
    tally = tally.T

    lanes_ref[...] = jnp.zeros_like(lanes_ref)
    for e in range(every):
        if e < GHOST:
            block = low_ref[:, e * PTS:(e + 1) * PTS]
        elif e < GHOST + local:
            block = own_ref[:, (e - GHOST) * PTS:(e - GHOST + 1) * PTS]
        else:
            at = e - GHOST - local
            block = high_ref[:, at * PTS:(at + 1) * PTS]
        block = jnp.concatenate([block[:8] - shift_by, block[8:]], 0)
        shift = starts[e] & (PTS - 1)
        here = pl.multiple_of((starts[e] >> 7) << 7, PTS)
        after = pl.multiple_of(((starts[e] >> 7) + 1) << 7, PTS)
        rolled = pltpu.roll(block, shift, 1)
        keep = lane >= shift
        lanes_ref[:, pl.ds(here, PTS)] = jnp.where(keep, rolled, lanes_ref[:, pl.ds(here, PTS)])
        lanes_ref[:, pl.ds(after, PTS)] = jnp.where(keep, 0.0, rolled)
        if GHOST <= e < GHOST + local:
            col = jnp.broadcast_to(tally[:, e - GHOST:e - GHOST + 1], (every, PTS))
            here = pl.multiple_of(here - base, PTS)
            after = pl.multiple_of(after - base, PTS)
            mult_ref[:, pl.ds(here, PTS)] = jnp.where(keep, col, mult_ref[:, pl.ds(here, PTS)])
            mult_ref[:, pl.ds(after, PTS)] = col

    group = 4 * PTS
    head = starts[0] >> 7
    tail = (starts[every] + 127) >> 7

    def spread(i, _):
        at = pl.multiple_of((head + 4 * i) * PTS, PTS)
        pos = lanes_ref[0:8, pl.ds(at, group)]
        norm = pos[0:1] * pos[0:1] + pos[1:2] * pos[1:2] + pos[2:3] * pos[2:3]
        feats = jnp.concatenate([-2.0 * pos[0:3], norm + soften, pos[4:8]], 0)
        lanes_ref[3:4, pl.ds(at, group)] = norm
        turned = feats.T
        for k in range(4):
            src_ref[k, pl.ds(at, group), :] = jnp.broadcast_to(turned[:, k:k + 1], (group, PTS))
        chg = lanes_ref[8:8 + probes, pl.ds(at, group)]
        hi = chg.astype(bf16)
        chg_ref[0:probes, pl.ds(at, group)] = hi
        chg_ref[probes:2 * probes, pl.ds(at, group)] = (chg - hi.astype(f32)).astype(bf16)
        return 0

    lax.fori_loop(0, (tail - head + 3) // 4 + 1, spread, 0)

    def target_block(t, _):
        where = pl.multiple_of(t * 256, 256)
        tgt = lanes_ref[0:8, pl.ds(pl.multiple_of(base + where, 256), 256)]
        lo_row = (start_ref[from_ref[t] - GHOST] >> 7) << 7
        hi_row = start_ref[to_ref[t] + GHOST + 1]

        def chunk(row, size, carry):
            first_sum, second_sum = carry
            row = pl.multiple_of(row, PTS)
            his, los = [], []
            for r in range(size // 16):
                at = pl.multiple_of(row + 16 * r, 16)
                leaf = leaf_ref[(row >> 4) + r]
                weight = mult_ref[pl.ds(leaf, 1), pl.ds(where, 256)]
                hi_pair, lo_pair = [], []
                for half in range(2):
                    x = tgt[:, half * 128:(half + 1) * 128]
                    s = (src_ref[3, pl.ds(at, 16), :] + x[3:4]) + src_ref[0, pl.ds(at, 16), :] * x[0:1]
                    s = s + (src_ref[1, pl.ds(at, 16), :] * x[1:2] + src_ref[2, pl.ds(at, 16), :] * x[2:3])
                    k = lax.rsqrt(s) * weight[:, half * 128:(half + 1) * 128]
                    hi = k.astype(bf16)
                    hi_pair.append(hi)
                    lo_pair.append((k - hi.astype(f32)).astype(bf16))
                his.append(jnp.concatenate(hi_pair, 1))
                los.append(jnp.concatenate(lo_pair, 1))
            chg = chg_ref[:, pl.ds(row, size)]
            first_sum = first_sum + jnp.dot(chg, jnp.concatenate(his, 0), preferred_element_type=f32)
            second_sum = second_sum + jnp.dot(chg[:probes], jnp.concatenate(los, 0), preferred_element_type=f32)
            return first_sum, second_sum

        sums = (jnp.zeros((2 * probes, 256), f32), jnp.zeros((probes, 256), f32))
        size = 512
        sums = lax.fori_loop(0, (hi_row - lo_row + size - 1) // size, lambda i, c: chunk(lo_row + size * i, size, c), sums)
        res_ref[:, pl.ds(where, 256)] = sums[0][:probes] + sums[0][probes:] + sums[1]
        return 0

    lax.fori_loop(0, (starts[GHOST + local] - base + 255) // 256, target_block, 0)

    for g in range(local):
        at = starts[g + GHOST] - base
        shift = at & (PTS - 1)
        here = pl.multiple_of((at >> 7) << 7, PTS)
        after = pl.multiple_of(((at >> 7) + 1) << 7, PTS)
        back = (PTS - shift) & (PTS - 1)
        value = jnp.where(lane < PTS - shift, pltpu.roll(res_ref[:, pl.ds(here, PTS)], back, 1),
                          pltpu.roll(res_ref[:, pl.ds(after, PTS)], back, 1))
        out_ref[:, g * PTS:(g + 1) * PTS] = jnp.where(lane < counts_ref[g], value * inv_four_pi, 0.0)


def near_call(first, counts, own, low, high, u_list):
    local = counts.shape[0]
    probes = own.shape[0] - 8
    every = local + 2 * GHOST
    width = every * PTS + 8 * PTS + 512
    targets = local * PTS + 512
    smem = pl.BlockSpec(memory_space=pltpu.SMEM)
    vmem = pl.BlockSpec(memory_space=pltpu.VMEM)
    return pl.pallas_call(
        near_kernel,
        out_shape=jax.ShapeDtypeStruct((probes, local * PTS), jnp.float32),
        in_specs=[smem, smem, vmem, vmem, vmem, vmem],
        out_specs=vmem,
        scratch_shapes=[
            pltpu.VMEM((8 + probes, width), jnp.float32),
            pltpu.VMEM((2 * probes, width), jnp.bfloat16),
            pltpu.VMEM((4, width, PTS), jnp.float32),
            pltpu.VMEM((every, targets), jnp.float32),
            pltpu.VMEM((probes, targets), jnp.float32),
            pltpu.SMEM((every + 1,), jnp.int32),
            pltpu.SMEM((width // 16 + 64,), jnp.int32),
            pltpu.SMEM((local * PTS // 256 + 1,), jnp.int32),
            pltpu.SMEM((local * PTS // 256 + 1,), jnp.int32),
        ],
        compiler_params=pltpu.CompilerParams(vmem_limit_bytes=48 << 20),
        cost_estimate=pl.CostEstimate(flops=4_000_000_000, bytes_accessed=2_000_000, transcendentals=4_000_000),
        name="near",
    )(first, counts, own, low, high, u_list)


def shards(offsets, charges, counts, u_list, v_src, v_type, wanted, m2l, uc2e, dc2e):
    local_leaves = counts.shape[0]
    per_leaf = offsets.shape[1] // local_leaves
    probes = charges.shape[0]
    equiv = uc2e.shape[0]
    kinds_count = m2l.shape[1] // equiv
    m2l_ops = m2l.reshape(equiv, kinds_count, equiv)
    bits = lax.axis_size("cube").bit_length() - 1
    read_cap = wanted.shape[2]
    surface = jnp.asarray(surface_table())
    first = lax.axis_index("cube") * local_leaves
    leaf_ids = first + jnp.arange(local_leaves, dtype=jnp.int32)
    inside = (jnp.arange(per_leaf, dtype=jnp.int32)[None, :] < counts[:, None]).astype(jnp.float32)
    corners = leaf_corner(leaf_ids)
    centers = corners + 0.5
    points = offsets.reshape(3, local_leaves, per_leaf) + corners[:, :, None]
    masked = charges.reshape(probes, local_leaves, per_leaf) * inside[None]
    held = jnp.broadcast_to(counts.astype(jnp.float32)[:, None], (local_leaves, per_leaf))
    own = jnp.concatenate(
        [
            points.reshape(3, local_leaves * per_leaf),
            held.reshape(1, local_leaves * per_leaf),
            jnp.zeros((4, local_leaves * per_leaf), jnp.float32),
            masked.reshape(probes, local_leaves * per_leaf),
        ],
        0,
    )
    low, high = halo(own, "cube", GHOST * per_leaf)
    up_flat = upward(points, masked, centers, surface, uc2e).reshape(local_leaves, probes * equiv)
    pieces = []
    for bit_num in range(bits):
        pieces.append(from_partner(up_flat, "cube", bit_num))
    table = jnp.concatenate(pieces + [up_flat], 0)
    bit_part = jnp.minimum(v_src // read_cap, bits - 1)
    slot_part = v_src % read_cap
    remote_leaf = wanted[0][bit_part, slot_part]
    rows = jnp.where(
        v_src >= bits * read_cap,
        bits * local_leaves + v_src - bits * read_cap,
        bit_part * local_leaves + remote_leaf,
    )
    row_ids = jnp.arange(table.shape[0], dtype=jnp.int32)
    type_ids = jnp.arange(kinds_count, dtype=jnp.int32)
    onehot_rows = (rows[:, :, None] == row_ids[None, None, :]).astype(jnp.float32)
    onehot_types = (v_type[:, :, None] == type_ids[None, None, :]).astype(jnp.float32)
    tally = jnp.einsum("lvr,lvt->ltr", onehot_rows, onehot_types)
    by_type = jnp.einsum("ltr,rc->ltc", tally, table, precision=highest)
    by_type = by_type.reshape(local_leaves, kinds_count, probes, equiv)
    downcheck = jnp.einsum("ltqj,itj->lqi", by_type, m2l_ops, precision=highest)
    far = downward(points, centers, surface, downcheck, dc2e)
    near = near_call(first.reshape(1).astype(jnp.int32), counts, own, low, high, u_list)
    potential = near + (far * inside[None]).reshape(probes, local_leaves * per_leaf)
    return potential


def solution(mesh):
    in_specs = (
        P(None, "cube"),
        P(None, "cube"),
        P("cube"),
        P("cube", None),
        P("cube", None),
        P("cube", None),
        P("cube", None, None),
        P(),
        P(),
        P(),
    )
    out_specs = P(None, "cube")
    return jax.shard_map(shards, mesh=mesh, in_specs=in_specs, out_specs=out_specs, check_vma=False)
```

```python
import math

import jax
import jax.numpy as jnp
import numpy as np
from jax import lax
from jax.experimental import pallas as pl
from jax.experimental.pallas import tpu as pltpu
from jax.sharding import PartitionSpec as P

GHOST = 8
PTS = 128


soften = 0.01
inv_four_pi = 1.0 / (4.0 * math.pi)
surface_radius = 0.55
highest = lax.Precision.HIGHEST


def from_partner(array, axis, bit):
    return lax.ppermute(array, axis, [(i, i ^ 1 << bit) for i in range(lax.axis_size(axis))])


def surface_table():
    lattice = np.arange(6)
    coords = np.stack(np.meshgrid(lattice, lattice, lattice, indexing="ij"), 0).reshape(3, -1)
    coords = (coords - 2.5) / 2.5
    on_face = np.max(np.abs(coords), axis=0) > 0.99
    return coords[:, on_face].astype(np.float32)


def near_kernel(first_ref, counts_ref, own_ref, low_ref, high_ref, ulist_ref, out_ref,
                lanes_ref, chg_ref, src_ref, mult_ref, res_ref, start_ref, leaf_ref, from_ref, to_ref):
    f32, bf16, i32 = jnp.float32, jnp.bfloat16, jnp.int32
    local = out_ref.shape[1] // PTS
    every = local + 2 * GHOST
    probes = out_ref.shape[0]
    base = GHOST * PTS
    lane = lax.broadcasted_iota(i32, (1, PTS), 1)

    first = first_ref[0]
    centre = []
    for axis in range(3):
        low = high = jnp.int32(0)
        for digit in range(10):
            low = low + (((first >> (3 * digit + axis)) & 1) << digit)
            high = high + ((((first + local - 1) >> (3 * digit + axis)) & 1) << digit)
        centre.append((low + high + 1).astype(f32) * 0.5)
    sub = lax.broadcasted_iota(i32, (8, PTS), 0)
    shift_by = jnp.where(sub == 0, centre[0], jnp.where(sub == 1, centre[1], jnp.where(sub == 2, centre[2], 0.0)))

    def units(n):
        return ((n + 15) // 16) * 16

    def ghost_count(ref, e):
        return jnp.max(ref[3:4, e * PTS:(e + 1) * PTS]).astype(i32)

    starts = [None] * (every + 1)
    starts[GHOST] = jnp.int32(base)
    for e in range(GHOST - 1, -1, -1):
        starts[e] = starts[e + 1] - units(ghost_count(low_ref, e))
    for e in range(GHOST, GHOST + local):
        starts[e + 1] = starts[e] + units(counts_ref[e - GHOST])
    for e in range(GHOST + local, every):
        starts[e + 1] = starts[e] + units(ghost_count(high_ref, e - GHOST - local))
    for e in range(every + 1):
        start_ref[e] = starts[e]

    for i in range(8):
        leaf_ref[jnp.maximum((starts[0] >> 4) - 8 + i, 0)] = 0
    for e in range(every):
        for i in range(8 if e < every - 1 else 48):
            leaf_ref[(starts[e] >> 4) + i] = e

    for e in range(GHOST, GHOST + local):
        head = starts[e] - base
        tail = starts[e + 1] - base - 1
        @pl.when(tail >= head)
        def _():
            h, t = head >> 8, tail >> 8

            @pl.when((head & 255) == 0)
            def _():
                from_ref[h] = e

            @pl.when(t > h)
            def _():
                from_ref[t] = e

            to_ref[h] = e
            to_ref[t] = e

    ids = ulist_ref[...] - (first - GHOST)
    which = lax.broadcasted_iota(i32, (local, every), 1)
    tally = jnp.zeros((local, every), f32)
    for u in range(ids.shape[1]):
        tally = tally + (ids[:, u:u + 1] == which).astype(f32)
    tally = tally.T

    lanes_ref[...] = jnp.zeros_like(lanes_ref)
    for e in range(every):
        if e < GHOST:
            block = low_ref[:, e * PTS:(e + 1) * PTS]
        elif e < GHOST + local:
            block = own_ref[:, (e - GHOST) * PTS:(e - GHOST + 1) * PTS]
        else:
            at = e - GHOST - local
            block = high_ref[:, at * PTS:(at + 1) * PTS]
        block = jnp.concatenate([block[:8] - shift_by, block[8:]], 0)
        shift = starts[e] & (PTS - 1)
        here = pl.multiple_of((starts[e] >> 7) << 7, PTS)
        after = pl.multiple_of(((starts[e] >> 7) + 1) << 7, PTS)
        rolled = pltpu.roll(block, shift, 1)
        keep = lane >= shift
        lanes_ref[:, pl.ds(here, PTS)] = jnp.where(keep, rolled, lanes_ref[:, pl.ds(here, PTS)])
        lanes_ref[:, pl.ds(after, PTS)] = jnp.where(keep, 0.0, rolled)
        if GHOST <= e < GHOST + local:
            col = jnp.broadcast_to(tally[:, e - GHOST:e - GHOST + 1], (every, PTS))
            here = pl.multiple_of(here - base, PTS)
            after = pl.multiple_of(after - base, PTS)
            mult_ref[:, pl.ds(here, PTS)] = jnp.where(keep, col, mult_ref[:, pl.ds(here, PTS)])
            mult_ref[:, pl.ds(after, PTS)] = col

    group = 4 * PTS
    head = starts[0] >> 7
    tail = (starts[every] + 127) >> 7

    def spread(i, _):
        at = pl.multiple_of((head + 4 * i) * PTS, PTS)
        pos = lanes_ref[0:8, pl.ds(at, group)]
        norm = pos[0:1] * pos[0:1] + pos[1:2] * pos[1:2] + pos[2:3] * pos[2:3]
        feats = jnp.concatenate([-2.0 * pos[0:3], norm + soften, pos[4:8]], 0)
        lanes_ref[3:4, pl.ds(at, group)] = norm
        turned = feats.T
        for k in range(4):
            src_ref[k, pl.ds(at, group), :] = jnp.broadcast_to(turned[:, k:k + 1], (group, PTS))
        chg = lanes_ref[8:8 + probes, pl.ds(at, group)]
        hi = chg.astype(bf16)
        chg_ref[0:probes, pl.ds(at, group)] = hi
        chg_ref[probes:2 * probes, pl.ds(at, group)] = (chg - hi.astype(f32)).astype(bf16)
        return 0

    lax.fori_loop(0, (tail - head + 3) // 4 + 1, spread, 0)

    def target_block(t, _):
        where = pl.multiple_of(t * 256, 256)
        tgt = lanes_ref[0:8, pl.ds(pl.multiple_of(base + where, 256), 256)]
        lo_row = (start_ref[from_ref[t] - GHOST] >> 7) << 7
        hi_row = start_ref[to_ref[t] + GHOST + 1]

        def chunk(row, size, carry):
            first_sum, second_sum = carry
            row = pl.multiple_of(row, PTS)
            his, los = [], []
            for r in range(size // 16):
                at = pl.multiple_of(row + 16 * r, 16)
                leaf = leaf_ref[(row >> 4) + r]
                weight = mult_ref[pl.ds(leaf, 1), pl.ds(where, 256)]
                hi_pair, lo_pair = [], []
                for half in range(2):
                    x = tgt[:, half * 128:(half + 1) * 128]
                    s = (src_ref[3, pl.ds(at, 16), :] + x[3:4]) + src_ref[0, pl.ds(at, 16), :] * x[0:1]
                    s = s + (src_ref[1, pl.ds(at, 16), :] * x[1:2] + src_ref[2, pl.ds(at, 16), :] * x[2:3])
                    k = lax.rsqrt(s) * weight[:, half * 128:(half + 1) * 128]
                    hi = k.astype(bf16)
                    hi_pair.append(hi)
                    lo_pair.append((k - hi.astype(f32)).astype(bf16))
                his.append(jnp.concatenate(hi_pair, 1))
                los.append(jnp.concatenate(lo_pair, 1))
            chg = chg_ref[:, pl.ds(row, size)]
            first_sum = first_sum + jnp.dot(chg, jnp.concatenate(his, 0), preferred_element_type=f32)
            second_sum = second_sum + jnp.dot(chg[:probes], jnp.concatenate(los, 0), preferred_element_type=f32)
            return first_sum, second_sum

        sums = (jnp.zeros((2 * probes, 256), f32), jnp.zeros((probes, 256), f32))
        size = 512
        sums = lax.fori_loop(0, (hi_row - lo_row + size - 1) // size, lambda i, c: chunk(lo_row + size * i, size, c), sums)
        res_ref[:, pl.ds(where, 256)] = sums[0][:probes] + sums[0][probes:] + sums[1]
        return 0

    lax.fori_loop(0, (starts[GHOST + local] - base + 255) // 256, target_block, 0)

    for g in range(local):
        at = starts[g + GHOST] - base
        shift = at & (PTS - 1)
        here = pl.multiple_of((at >> 7) << 7, PTS)
        after = pl.multiple_of(((at >> 7) + 1) << 7, PTS)
        back = (PTS - shift) & (PTS - 1)
        value = jnp.where(lane < PTS - shift, pltpu.roll(res_ref[:, pl.ds(here, PTS)], back, 1),
                          pltpu.roll(res_ref[:, pl.ds(after, PTS)], back, 1))
        out_ref[:, g * PTS:(g + 1) * PTS] = jnp.where(lane < counts_ref[g], value * inv_four_pi, 0.0)


def near_call(first, counts, own, low, high, u_list):
    local = counts.shape[0]
    probes = own.shape[0] - 8
    every = local + 2 * GHOST
    width = every * PTS + 8 * PTS + 512
    targets = local * PTS + 512
    smem = pl.BlockSpec(memory_space=pltpu.SMEM)
    vmem = pl.BlockSpec(memory_space=pltpu.VMEM)
    return pl.pallas_call(
        near_kernel,
        out_shape=jax.ShapeDtypeStruct((probes, local * PTS), jnp.float32),
        in_specs=[smem, smem, vmem, vmem, vmem, vmem],
        out_specs=vmem,
        scratch_shapes=[
            pltpu.VMEM((8 + probes, width), jnp.float32),
            pltpu.VMEM((2 * probes, width), jnp.bfloat16),
            pltpu.VMEM((4, width, PTS), jnp.float32),
            pltpu.VMEM((every, targets), jnp.float32),
            pltpu.VMEM((probes, targets), jnp.float32),
            pltpu.SMEM((every + 1,), jnp.int32),
            pltpu.SMEM((width // 16 + 64,), jnp.int32),
            pltpu.SMEM((local * PTS // 256 + 1,), jnp.int32),
            pltpu.SMEM((local * PTS // 256 + 1,), jnp.int32),
        ],
        compiler_params=pltpu.CompilerParams(vmem_limit_bytes=48 << 20),
        cost_estimate=pl.CostEstimate(flops=4_000_000_000, bytes_accessed=2_000_000, transcendentals=4_000_000),
        name="near",
    )(first, counts, own, low, high, u_list)


def split(value):
    high = value.astype(jnp.bfloat16)
    return high, (value - high.astype(jnp.float32)).astype(jnp.bfloat16)


def dot(left, right):
    return jnp.dot(left, right, preferred_element_type=jnp.float32)


def dot_t(left, right):
    return lax.dot_general(left, right, (((1,), (1,)), ((), ())), preferred_element_type=jnp.float32)


def dot_t3(left, right):
    left_hi, left_lo = split(left)
    right_hi, right_lo = split(right)
    return dot_t(left_hi, right_hi) + (dot_t(left_hi, right_lo) + dot_t(left_lo, right_hi))


def corner_of(leaf, axis):
    summed = jnp.int32(0)
    for digit in range(10):
        summed = summed + (((leaf >> (3 * digit + axis)) & 1) << digit)
    return summed.astype(jnp.float32)


def surface_tile(local, surface):
    norm = local[0:1] * local[0:1] + (local[1:2] * local[1:2] + local[2:3] * local[2:3])
    s = (norm + surface[:, 3:4]) + surface[:, 0:1] * local[0:1]
    s = s + (surface[:, 1:2] * local[1:2] + surface[:, 2:3] * local[2:3])
    return lax.rsqrt(s)


def surface_rows():
    points = surface_radius * surface_table().astype(np.float64)
    count = points.shape[1]
    rows = np.zeros((-(-count // 16) * 16, 8), np.float32)
    rows[:count, :3] = -2.0 * points.T
    rows[:count, 3] = (points ** 2).sum(0) + soften
    rows[count:, 3] = 1.0
    return rows


def padded(ref, rows, lanes):
    value = ref[...]
    if value.shape[1] < lanes:
        value = jnp.concatenate([value, jnp.zeros((value.shape[0], lanes - value.shape[1]), value.dtype)], 1)
    if value.shape[0] < rows:
        value = jnp.concatenate([value, jnp.zeros((rows - value.shape[0], lanes), value.dtype)], 0)
    return value


def up_kernel(first_ref, counts_ref, offsets_ref, charges_ref, uc2e_ref, surface_ref,
              own_ref, low_ref, high_ref, up_ref, check_ref):
    f32, i32 = jnp.float32, jnp.int32
    probes, points = charges_ref.shape
    local = points // PTS
    lane = lax.broadcasted_iota(i32, (1, PTS), 1)
    sub = lax.broadcasted_iota(i32, (8, PTS), 0)
    first = first_ref[0]
    surface = surface_ref[...]
    zero = jnp.zeros((probes, PTS), jnp.bfloat16)

    for g in range(0, local, 2):
        parts = []
        for h in (g, g + 1):
            at = slice(h * PTS, (h + 1) * PTS)
            corner = [corner_of(first + h, axis) for axis in range(3)]
            held = counts_ref[h]
            xyz = jnp.concatenate([offsets_ref[:, at], jnp.zeros((5, PTS), f32)], 0)
            move = jnp.where(sub == 0, corner[0], jnp.where(sub == 1, corner[1], jnp.where(sub == 2, corner[2],
                   jnp.where(sub == 3, held.astype(f32), 0.0))))
            own_ref[0:8, at] = xyz + move
            masked = jnp.where(lane < held, charges_ref[:, at], 0.0)
            own_ref[8:8 + probes, at] = masked
            parts.append(split(masked))
        both = offsets_ref[:, g * PTS:(g + 2) * PTS] - 0.5
        tile_hi, tile_lo = split(surface_tile(both, surface))
        left = jnp.concatenate([parts[0][0], zero], 1), jnp.concatenate([zero, parts[1][0]], 1)
        small = jnp.concatenate([parts[0][1], zero], 1), jnp.concatenate([zero, parts[1][1]], 1)
        large = dot_t(jnp.concatenate(left + small, 0), tile_hi)
        fine = dot_t(jnp.concatenate(left, 0), tile_lo)
        value = (large[:2 * probes] + (large[2 * probes:] + fine)) * inv_four_pi
        gap = jnp.zeros((2 * probes, 2 * PTS - value.shape[1]), f32)
        value = jnp.concatenate([value, gap], 1)
        for half in range(2):
            at = slice(half * PTS, (half + 1) * PTS)
            check_ref[half, pl.ds(g, probes, stride=local), :] = value[:probes, at]
            check_ref[half, pl.ds(g + 1, probes, stride=local), :] = value[probes:, at]
    low_ref[...] = own_ref[:, points - GHOST * PTS:]
    high_ref[...] = own_ref[:, :GHOST * PTS]

    equiv = uc2e_ref.shape[0]
    up = dot_t3(jnp.concatenate([check_ref[0], check_ref[1]], 1), padded(uc2e_ref, 2 * PTS, 2 * PTS))
    rows = probes * local
    up_ref[:rows] = up[:, :PTS]
    rest = rows // 4
    tail = up[:rest, PTS:]
    for k in range(1, 4):
        tail = tail + pltpu.roll(up[k * rest:(k + 1) * rest, PTS:], 32 * k, 1)
    up_ref[rows:] = tail


def up_call(first, counts, offsets, charges, uc2e):
    local = counts.shape[0]
    probes, points = charges.shape
    smem = pl.BlockSpec(memory_space=pltpu.SMEM)
    vmem = pl.BlockSpec(memory_space=pltpu.VMEM)
    f32 = jnp.float32
    return pl.pallas_call(
        up_kernel,
        out_shape=(
            jax.ShapeDtypeStruct((8 + probes, points), f32),
            jax.ShapeDtypeStruct((8 + probes, GHOST * PTS), f32),
            jax.ShapeDtypeStruct((8 + probes, GHOST * PTS), f32),
            jax.ShapeDtypeStruct((probes * local * 5 // 4, PTS), f32),
        ),
        in_specs=[smem, smem, vmem, vmem, vmem, vmem],
        out_specs=(vmem, vmem, vmem, vmem),
        scratch_shapes=[pltpu.VMEM((2, probes * local, PTS), f32)],
        compiler_params=pltpu.CompilerParams(vmem_limit_bytes=32 << 20),
        cost_estimate=pl.CostEstimate(flops=500_000_000, bytes_accessed=1_500_000, transcendentals=600_000),
        name="upward",
    )(first, counts, offsets, charges, uc2e, jnp.asarray(surface_rows()))


def far_kernel(counts_ref, wanted_ref, offsets_ref, near_ref, vsrc_ref, vtype_ref, m2l_ref, dc2e_ref, surface_ref,
               *refs):
    f32, bf16, i32 = jnp.float32, jnp.bfloat16, jnp.int32
    pieces = refs[:-9]
    out_ref, code_ref, tally_ref, table_ref, x_hi_ref, x_lo_ref, w_hi_ref, w_lo_ref, eq_ref = refs[-9:]
    probes, points = out_ref.shape
    local = points // PTS
    bits, cap = wanted_ref.shape
    depth = len(pieces) * local
    equiv = m2l_ref.shape[0]
    kinds = m2l_ref.shape[1] // equiv
    rest = equiv - PTS
    rows = probes * local
    lane = lax.broadcasted_iota(i32, (1, PTS), 1)

    w_hi_ref[...] = jnp.zeros_like(w_hi_ref)
    w_lo_ref[...] = jnp.zeros_like(w_lo_ref)
    grown = w_hi_ref.shape[0]
    fill = jnp.zeros((grown - equiv, PTS), f32)
    for t in range(kinds):
        main = jnp.concatenate([m2l_ref[:, t * equiv:t * equiv + PTS], fill], 0)
        w_hi_ref[:, t * PTS:(t + 1) * PTS], w_lo_ref[:, t * PTS:(t + 1) * PTS] = split(main)
    gap = jnp.zeros((equiv, 32 - rest), f32)
    for t in range(0, kinds, 4):
        row = []
        for k in range(4):
            row += [m2l_ref[:, (t + k) * equiv + PTS:(t + k + 1) * equiv], gap]
        tail = jnp.concatenate([jnp.concatenate(row, 1), fill], 0)
        at = kinds * PTS + t * 32
        w_hi_ref[:, at:at + PTS], w_lo_ref[:, at:at + PTS] = split(tail)

    codes = vsrc_ref[...]
    slots = codes.shape[1]
    found = codes - bits * cap + bits * local
    for b in range(bits):
        for s in range(cap):
            found = jnp.where(codes == b * cap + s, b * local + wanted_ref[b, s], found)
    code_ref[...] = jnp.full(code_ref.shape, -1.0, f32)
    code_ref[0:local, 0:slots] = found.astype(f32)
    code_ref[local:, 0:slots] = vtype_ref[...].astype(f32)

    per = PTS // slots
    spot = lax.broadcasted_iota(i32, (8, 8 * slots), 1) // slots == lax.broadcasted_iota(i32, (8, 8 * slots), 0)

    def flat(value):
        wide = jnp.where(lane < slots, value, 0.0)
        total = wide
        for k in range(1, per):
            total = total + pltpu.roll(wide, slots * k, 1)
        total = jnp.concatenate([total] * (8 // per), 1)
        return jnp.sum(jnp.where(spot, total, 0.0), 0, keepdims=True)

    row_id = lax.broadcasted_iota(i32, (8 * kinds, 8 * slots), 0)
    mine = lax.broadcasted_iota(i32, (8 * kinds, 8 * slots), 1) // slots == row_id % 8
    kind = (row_id // 8).astype(f32)
    table_row = lax.broadcasted_iota(i32, (depth, 8 * slots), 0).astype(f32)
    for g in range(0, local, 8):
        take = flat(code_ref[g:g + 8, :])
        sort = flat(code_ref[local + g:local + g + 8, :])
        pick = jnp.where(mine & (sort == kind), 1.0, 0.0).astype(bf16)
        hit = jnp.where(take == table_row, 1.0, 0.0).astype(bf16)
        count = dot_t(pick, hit)
        for t in range(kinds):
            tally_ref[t * local + g:t * local + g + 8, :] = count[8 * t:8 * t + 8]
    tally = tally_ref[...].astype(bf16)

    blocks = pieces[0].shape[0] // local
    for b, piece in enumerate(pieces):
        for n in range(blocks):
            hi, lo = split(piece[n * local:(n + 1) * local, :])
            table_ref[b * local:(b + 1) * local, n * PTS:(n + 1) * PTS] = hi
            table_ref[depth + b * local:depth + (b + 1) * local, n * PTS:(n + 1) * PTS] = lo

    twice = jnp.concatenate([tally, tally], 1)
    group = lane // 32
    quarter = probes // 4
    for n in range(0, blocks, 2):
        both = dot(twice, table_ref[:, n * PTS:(n + 2) * PTS])
        for half in range(2):
            q = n + half
            part = both[:, half * PTS:(half + 1) * PTS]
            if q < probes:
                hi, lo = split(part)
                for t in range(kinds):
                    x_hi_ref[q * local:(q + 1) * local, t * PTS:(t + 1) * PTS] = hi[t * local:(t + 1) * local]
                    x_lo_ref[q * local:(q + 1) * local, t * PTS:(t + 1) * PTS] = lo[t * local:(t + 1) * local]
            else:
                for k in range(4):
                    to = (q - probes + quarter * k) * local
                    for t in range(0, kinds, 4):
                        value = jnp.zeros((local, PTS), f32)
                        for i in range(4):
                            moved = part[(t + i) * local:(t + i + 1) * local]
                            if i != k:
                                moved = pltpu.roll(moved, (32 * (i - k)) % PTS, 1)
                            value = jnp.where(group == i, moved, value)
                        at = kinds * PTS + t * 32
                        x_hi_ref[to:to + local, at:at + PTS], x_lo_ref[to:to + local, at:at + PTS] = split(value)

    down = dot_t(x_hi_ref[...], w_hi_ref[...]) + (dot_t(x_hi_ref[...], w_lo_ref[...]) + dot_t(x_lo_ref[...], w_hi_ref[...]))
    equivs = dot_t3(down, padded(dc2e_ref, 2 * PTS, 2 * PTS))
    eq_ref[0], eq_ref[1] = equivs[:, :PTS], equivs[:, PTS:]

    surface = surface_ref[...]
    reach = surface.shape[0]
    for g in range(0, local, 2):
        at = slice(g * PTS, (g + 2) * PTS)
        tile_hi, tile_lo = split(surface_tile(offsets_ref[:, at] - 0.5, surface))
        parts = []
        for h in (g, g + 1):
            value = jnp.concatenate([eq_ref[half, pl.ds(h, probes, stride=local), :] for half in range(2)], 1)[:, :reach]
            parts.append(split(value))
        left = parts[0][0], parts[1][0]
        large = dot(jnp.concatenate(left + (parts[0][1], parts[1][1]), 0), tile_hi)
        value = large[:2 * probes] + (large[2 * probes:] + dot(jnp.concatenate(left, 0), tile_lo))
        for i in range(2):
            h = g + i
            to = slice(h * PTS, (h + 1) * PTS)
            part = value[i * probes:(i + 1) * probes, i * PTS:(i + 1) * PTS] * inv_four_pi
            out_ref[:, to] = jnp.where(lane < counts_ref[h], near_ref[:, to] + part, 0.0)


def far_call(counts, wanted, offsets, near, v_src, v_type, m2l, dc2e, pieces):
    local = counts.shape[0]
    probes, points = near.shape
    equiv = dc2e.shape[0]
    kinds = m2l.shape[1] // equiv
    smem = pl.BlockSpec(memory_space=pltpu.SMEM)
    vmem = pl.BlockSpec(memory_space=pltpu.VMEM)
    f32, bf16 = jnp.float32, jnp.bfloat16
    rows = probes * local
    wide = kinds * (PTS + 32)
    return pl.pallas_call(
        far_kernel,
        out_shape=jax.ShapeDtypeStruct((probes, points), f32),
        in_specs=[smem, smem] + [vmem] * (7 + len(pieces)),
        out_specs=vmem,
        scratch_shapes=[
            pltpu.VMEM((2 * local, PTS), f32),
            pltpu.VMEM((kinds * local, len(pieces) * local), f32),
            pltpu.VMEM((2 * len(pieces) * local, pieces[0].shape[0] // local * PTS), bf16),
            pltpu.VMEM((rows, wide), bf16),
            pltpu.VMEM((rows, wide), bf16),
            pltpu.VMEM((2 * PTS, wide), bf16),
            pltpu.VMEM((2 * PTS, wide), bf16),
            pltpu.VMEM((2, rows, PTS), f32),
        ],
        compiler_params=pltpu.CompilerParams(vmem_limit_bytes=40 << 20),
        cost_estimate=pl.CostEstimate(flops=4_000_000_000, bytes_accessed=4_000_000, transcendentals=600_000),
        name="far",
    )(counts, wanted, offsets, near, v_src, v_type, m2l, dc2e, jnp.asarray(surface_rows()), *pieces)


def shards(offsets, charges, counts, u_list, v_src, v_type, wanted, m2l, uc2e, dc2e):
    local_leaves = counts.shape[0]
    first = (lax.axis_index("cube") * local_leaves).astype(jnp.int32).reshape(1)
    own, to_next, to_last, up = up_call(first, counts, offsets, charges, uc2e)
    count = lax.axis_size("cube")
    forward = [(i, i + 1) for i in range(count - 1)]
    backward = [(target, source) for source, target in forward]
    low = lax.ppermute(to_next, "cube", forward)
    high = lax.ppermute(to_last, "cube", backward)
    pieces = [from_partner(up, "cube", bit) for bit in range(count.bit_length() - 1)] + [up]
    near = near_call(first, counts, own, low, high, u_list)
    return far_call(counts, wanted[0], offsets, near, v_src, v_type, m2l, dc2e, pieces)


def solution(mesh):
    in_specs = (
        P(None, "cube"),
        P(None, "cube"),
        P("cube"),
        P("cube", None),
        P("cube", None),
        P("cube", None),
        P("cube", None, None),
        P(),
        P(),
        P(),
    )
    out_specs = P(None, "cube")
    return jax.shard_map(shards, mesh=mesh, in_specs=in_specs, out_specs=out_specs, check_vma=False)
```

```python
import math

import jax
import jax.numpy as jnp
import numpy as np
from jax import lax
from jax.experimental import pallas as pl
from jax.experimental.pallas import tpu as pltpu
from jax.sharding import PartitionSpec as P

GHOST = 8
PTS = 128
UNIT = 8
UNIT_LOG = 3
SIDE = 3


soften = 0.01
inv_four_pi = 1.0 / (4.0 * math.pi)
surface_radius = 0.55
highest = lax.Precision.HIGHEST


def from_partner(array, axis, bit):
    return lax.ppermute(array, axis, [(i, i ^ 1 << bit) for i in range(lax.axis_size(axis))])


def surface_table():
    lattice = np.arange(6)
    coords = np.stack(np.meshgrid(lattice, lattice, lattice, indexing="ij"), 0).reshape(3, -1)
    coords = (coords - 2.5) / 2.5
    on_face = np.max(np.abs(coords), axis=0) > 0.99
    return coords[:, on_face].astype(np.float32)


def corner_of(leaf, axis):
    summed = jnp.int32(0)
    for digit in range(10):
        summed = summed + (((leaf >> (3 * digit + axis)) & 1) << digit)
    return summed.astype(jnp.float32)


def near_kernel(first_ref, counts_ref, offsets_ref, charges_ref, pair_ref, odd_ref, ulist_ref, out_ref,
                ghost_ref,
                lanes_ref, chg_ref, src_ref, tgt_ref, square_ref, hi_ref, lo_ref, acc_ref,
                mult_ref, res_ref, start_ref, leaf_ref, from_ref, to_ref, open_ref, shut_ref):
    f32, bf16, i32 = jnp.float32, jnp.bfloat16, jnp.int32
    local = out_ref.shape[1] // PTS
    every = local + 2 * GHOST
    probes = out_ref.shape[0]
    base = GHOST * PTS
    lane = lax.broadcasted_iota(i32, (1, PTS), 1)

    first = first_ref[0]
    centre = []
    for axis in range(3):
        low = high = jnp.int32(0)
        for digit in range(10):
            low = low + (((first >> (3 * digit + axis)) & 1) << digit)
            high = high + ((((first + local - 1) >> (3 * digit + axis)) & 1) << digit)
        centre.append((low + high + 1).astype(f32) * 0.5)
    sub = lax.broadcasted_iota(i32, (8, PTS), 0)
    shift_by = jnp.where(sub == 0, centre[0], jnp.where(sub == 1, centre[1], jnp.where(sub == 2, centre[2], 0.0)))

    def units(n):
        return ((n + UNIT - 1) >> UNIT_LOG) << UNIT_LOG

    deep = 8 + probes
    even = lax.rem(lax.div(first, local), 2) == 0
    skip = pair_ref.shape[0] - GHOST * deep
    odd, pair = odd_ref[...], pair_ref[skip:]
    ghost_ref[0] = jnp.where(even, odd, pair)
    ghost_ref[1] = jnp.where(even, pair, odd)

    def ghost_count(side, e):
        return jnp.max(ghost_ref[side, e * deep + 3:e * deep + 4, :]).astype(i32)

    starts = [None] * (every + 1)
    starts[GHOST] = jnp.int32(base)
    for e in range(GHOST - 1, -1, -1):
        starts[e] = starts[e + 1] - units(ghost_count(0, e))
    for e in range(GHOST, GHOST + local):
        starts[e + 1] = starts[e] + units(counts_ref[e - GHOST])
    for e in range(GHOST + local, every):
        starts[e + 1] = starts[e] + units(ghost_count(1, e - GHOST - local))
    for e in range(every + 1):
        start_ref[e] = starts[e]

    per = PTS // UNIT
    for i in range(per):
        leaf_ref[jnp.maximum((starts[0] >> UNIT_LOG) - per + i, 0)] = 0
    for e in range(every):
        for i in range(per if e < every - 1 else 6 * per):
            leaf_ref[(starts[e] >> UNIT_LOG) + i] = e

    for e in range(GHOST + local - 1, GHOST - 1, -1):
        from_ref[(starts[e + 1] - base - 1) >> 8] = e
        from_ref[(starts[e] - base) >> 8] = e
    for e in range(GHOST, GHOST + local):
        to_ref[(starts[e] - base) >> 8] = e
        to_ref[(starts[e + 1] - base - 1) >> 8] = e

    ids = ulist_ref[...] - (first - GHOST)
    which = lax.broadcasted_iota(i32, (local, every), 1)
    tally = jnp.zeros((local, every), f32)
    for u in range(ids.shape[1]):
        tally = tally + (ids[:, u:u + 1] == which).astype(f32)
    tally = tally.T

    lanes_ref[...] = jnp.zeros_like(lanes_ref)
    for e in range(every):
        if e < GHOST:
            block = ghost_ref[0, e * deep:(e + 1) * deep, :]
        elif e < GHOST + local:
            h = e - GHOST
            at = slice(h * PTS, (h + 1) * PTS)
            corner = [corner_of(first + h, axis) for axis in range(3)]
            move = jnp.where(sub == 0, corner[0], jnp.where(sub == 1, corner[1], corner[2]))
            xyz = jnp.concatenate([offsets_ref[:, at], jnp.zeros((5, PTS), f32)], 0)
            block = jnp.concatenate([xyz + move, jnp.where(lane < counts_ref[h], charges_ref[:, at], 0.0)], 0)
        else:
            at = e - GHOST - local
            block = ghost_ref[1, at * deep:(at + 1) * deep, :]
        block = jnp.concatenate([block[:8] - shift_by, block[8:]], 0)
        shift = starts[e] & (PTS - 1)
        here = pl.multiple_of((starts[e] >> 7) << 7, PTS)
        after = pl.multiple_of(((starts[e] >> 7) + 1) << 7, PTS)
        rolled = pltpu.roll(block, shift, 1)
        keep = lane >= shift
        lanes_ref[:, pl.ds(here, PTS)] = jnp.where(keep, rolled, lanes_ref[:, pl.ds(here, PTS)])
        lanes_ref[:, pl.ds(after, PTS)] = jnp.where(keep, 0.0, rolled)
        if GHOST <= e < GHOST + local:
            col = jnp.broadcast_to(tally[:, e - GHOST:e - GHOST + 1], (every, PTS))
            here = pl.multiple_of(((starts[e] - base) >> 7) * every, 8)
            after = pl.multiple_of((((starts[e] - base) >> 7) + 1) * every, 8)
            mult_ref[pl.ds(here, every), :] = jnp.where(keep, col, mult_ref[pl.ds(here, every), :])
            mult_ref[pl.ds(after, every), :] = col

    group = 4 * PTS
    head = starts[0] >> 7
    tail = (starts[every] + 127) >> 7
    row_id = lax.broadcasted_iota(i32, (8, group), 0)

    def spread(i, _):
        at = pl.multiple_of((head + 4 * i) * PTS, PTS)
        pos = jnp.where(row_id < 3, lanes_ref[0:8, pl.ds(at, group)], 0.0)
        pos_hi = pos.astype(bf16).astype(f32)
        pos_lo = (pos - pos_hi).astype(bf16).astype(f32)
        used = pos_hi + pos_lo
        norm = jnp.sum(used * used, 0, keepdims=True)

        def rows(blocks, total, three, four):
            parts = []
            for block in blocks[:3]:
                piece = total.astype(bf16).astype(f32)
                total = total - piece
                extra = jnp.where(row_id == three, piece, jnp.where(row_id == four, 1.0, 0.0))
                parts.append(jnp.where(row_id < 3, block, extra))
            return jnp.concatenate(parts + [blocks[3]], 0)

        src = rows((-2.0 * pos_hi, -2.0 * pos_hi, -2.0 * pos_lo, -2.0 * pos_lo), norm + soften, 3, 4)
        tgt = rows((pos_hi, pos_lo, pos_hi, pos_lo), norm, 4, 3)
        src_ref[pl.ds(at, group), :] = src.T.astype(bf16)
        tgt_ref[:, pl.ds(at, group)] = tgt.astype(bf16)
        chg = lanes_ref[8:8 + probes, pl.ds(at, group)]
        hi = chg.astype(bf16)
        chg_ref[0:probes, pl.ds(at, group)] = hi
        chg_ref[probes:2 * probes, pl.ds(at, group)] = (chg - hi.astype(f32)).astype(bf16)
        return 0

    lax.fori_loop(0, (tail - head + 5) // 4, spread, 0)

    acc_ref[...] = jnp.zeros_like(acc_ref)
    blocks = (starts[GHOST + local] - base + 255) >> 8
    steps = jnp.int32(0)
    for t in range(local * PTS // 256 + 1):
        real = t < blocks
        opens = (start_ref[jnp.where(real, from_ref[t], GHOST) - GHOST] >> 7) << 7
        shuts = jnp.where(real, start_ref[jnp.where(real, to_ref[t], GHOST) + GHOST + 1], 0)
        open_ref[t] = opens
        shut_ref[t] = shuts
        steps = steps + jnp.where(real, (shuts - opens + 255) >> 8, 0)

    def advance(step):
        t, row = step
        done = row + 256 >= shut_ref[t]
        after = jnp.minimum(jnp.where(done, t + 1, t), blocks)
        return after, jnp.where(done, open_ref[after], row + 256)

    def square(step, slot):
        t, row = step
        tgt = tgt_ref[:, pl.ds(pl.multiple_of(base + t * 256, 256), 256)]
        square_ref[slot] = jnp.dot(src_ref[pl.ds(pl.multiple_of(row, PTS), 256), :], tgt, preferred_element_type=f32)

    def weigh(step, slot):
        t, row = step
        left = t * (2 * every)
        for r in range(16):
            k = lax.rsqrt(square_ref[slot, 16 * r:16 * r + 16, :])
            parts = []
            for half in range(2):
                leaf = left + leaf_ref[(row >> UNIT_LOG) + 2 * r + half]
                weight = jnp.concatenate([mult_ref[pl.ds(leaf, 1), :], mult_ref[pl.ds(leaf + every, 1), :]], 1)
                parts.append(k[8 * half:8 * half + 8] * weight)
            k = jnp.concatenate(parts, 0)
            at = slice(16 * r, 16 * r + 16)
            hi = k.astype(bf16)
            hi_ref[slot, at, :] = hi
            lo_ref[slot, at, :] = (k - hi.astype(f32)).astype(bf16)

    def gather(step, slot):
        t, row = step
        where = pl.multiple_of(t * 256, 256)
        chg = chg_ref[:, pl.ds(pl.multiple_of(row, PTS), 256)]
        return (where, jnp.dot(chg, hi_ref[slot], preferred_element_type=f32),
                jnp.dot(chg[:probes], lo_ref[slot], preferred_element_type=f32))

    def add(where, first_sum, second_sum):
        acc_ref[0:2 * probes, pl.ds(where, 256)] += first_sum
        acc_ref[2 * probes:, pl.ds(where, 256)] += second_sum

    step = (jnp.int32(0), open_ref[0])
    order = [step]
    for _ in range(2 * SIDE - 1):
        step = advance(step)
        order.append(step)
    for c in range(SIDE):
        square(order[c], c)
    for c in range(SIDE):
        weigh(order[c], c)
    for c in range(SIDE):
        square(order[SIDE + c], c)

    def several(_, order):
        later = []
        step = order[-1]
        for c in range(SIDE):
            step = advance(step)
            later.append(step)
        sums = [gather(order[c], c) for c in range(SIDE)]
        for c in range(SIDE):
            weigh(order[SIDE + c], c)
        for c in range(SIDE):
            square(later[c], c)
        for each in sums:
            add(*each)
        return (*order[SIDE:], *later)

    lax.fori_loop(0, (steps + SIDE - 1) // SIDE, several, tuple(order))
    res_ref[...] = acc_ref[0:probes] + acc_ref[probes:2 * probes] + acc_ref[2 * probes:]

    for g in range(local):
        at = starts[g + GHOST] - base
        shift = at & (PTS - 1)
        here = pl.multiple_of((at >> 7) << 7, PTS)
        after = pl.multiple_of(((at >> 7) + 1) << 7, PTS)
        back = (PTS - shift) & (PTS - 1)
        value = jnp.where(lane < PTS - shift, pltpu.roll(res_ref[:, pl.ds(here, PTS)], back, 1),
                          pltpu.roll(res_ref[:, pl.ds(after, PTS)], back, 1))
        out_ref[:, g * PTS:(g + 1) * PTS] = jnp.where(lane < counts_ref[g], value * inv_four_pi, 0.0)


def near_call(first, counts, offsets, charges, pair, odd, u_list):
    local = counts.shape[0]
    probes = charges.shape[0]
    every = local + 2 * GHOST
    width = every * PTS + 8 * PTS + 512
    targets = local * PTS + 512
    smem = pl.BlockSpec(memory_space=pltpu.SMEM)
    vmem = pl.BlockSpec(memory_space=pltpu.VMEM)
    return pl.pallas_call(
        near_kernel,
        out_shape=jax.ShapeDtypeStruct((probes, local * PTS), jnp.float32),
        in_specs=[smem, smem, vmem, vmem, vmem, vmem, vmem],
        out_specs=vmem,
        scratch_shapes=[
            pltpu.VMEM((2, GHOST * (8 + probes), PTS), jnp.float32),
            pltpu.VMEM((8 + probes, width), jnp.float32),
            pltpu.VMEM((2 * probes, width), jnp.bfloat16),
            pltpu.VMEM((width, 32), jnp.bfloat16),
            pltpu.VMEM((32, width), jnp.bfloat16),
            pltpu.VMEM((SIDE, 256, 256), jnp.float32),
            pltpu.VMEM((SIDE, 256, 256), jnp.bfloat16),
            pltpu.VMEM((SIDE, 256, 256), jnp.bfloat16),
            pltpu.VMEM((3 * probes, targets), jnp.float32),
            pltpu.VMEM((targets // PTS * every, PTS), jnp.float32),
            pltpu.VMEM((probes, targets), jnp.float32),
            pltpu.SMEM((every + 1,), jnp.int32),
            pltpu.SMEM((width // UNIT + 64,), jnp.int32),
            pltpu.SMEM((local * PTS // 256 + 1,), jnp.int32),
            pltpu.SMEM((local * PTS // 256 + 1,), jnp.int32),
            pltpu.SMEM((local * PTS // 256 + 1,), jnp.int32),
            pltpu.SMEM((local * PTS // 256 + 1,), jnp.int32),
        ],
        compiler_params=pltpu.CompilerParams(vmem_limit_bytes=24 << 20),
        cost_estimate=pl.CostEstimate(flops=4_000_000_000, bytes_accessed=2_000_000, transcendentals=4_000_000),
        name="near",
    )(first, counts, offsets, charges, pair, odd, u_list)


def split(value):
    high = value.astype(jnp.bfloat16)
    return high, (value - high.astype(jnp.float32)).astype(jnp.bfloat16)


def dot(left, right):
    return jnp.dot(left, right, preferred_element_type=jnp.float32)


def dot_t(left, right):
    return lax.dot_general(left, right, (((1,), (1,)), ((), ())), preferred_element_type=jnp.float32)


def dot_t3(left, right):
    left_hi, left_lo = split(left)
    right_hi, right_lo = split(right)
    return dot_t(left_hi, right_hi) + (dot_t(left_hi, right_lo) + dot_t(left_lo, right_hi))


def surface_tile(local, surface):
    norm = local[0:1] * local[0:1] + (local[1:2] * local[1:2] + local[2:3] * local[2:3])
    s = (norm + surface[:, 3:4]) + surface[:, 0:1] * local[0:1]
    s = s + (surface[:, 1:2] * local[1:2] + surface[:, 2:3] * local[2:3])
    return lax.rsqrt(s)


def surface_rows():
    points = surface_radius * surface_table().astype(np.float64)
    count = points.shape[1]
    rows = np.zeros((-(-count // 16) * 16, 8), np.float32)
    rows[:count, :3] = -2.0 * points.T
    rows[:count, 3] = (points ** 2).sum(0) + soften
    rows[count:, 3] = 1.0
    return rows


def padded(ref, rows, lanes):
    value = ref[...]
    if value.shape[1] < lanes:
        value = jnp.concatenate([value, jnp.zeros((value.shape[0], lanes - value.shape[1]), value.dtype)], 1)
    if value.shape[0] < rows:
        value = jnp.concatenate([value, jnp.zeros((rows - value.shape[0], lanes), value.dtype)], 0)
    return value


def up_kernel(first_ref, counts_hbm, offsets_hbm, charges_hbm, uc2e_hbm, surface_hbm,
              odd_ref, pair_ref, up_ref, tile_hi_hbm, tile_lo_hbm,
              tile_hi_ref, tile_lo_ref, counts_ref, offsets_ref, charges_ref, uc2e_ref, surface_ref, check_ref, sems):
    f32, i32 = jnp.float32, jnp.int32
    copies = []
    for n, (source, target) in enumerate(((counts_hbm, counts_ref), (offsets_hbm, offsets_ref),
                                          (surface_hbm, surface_ref), (charges_hbm, charges_ref),
                                          (uc2e_hbm, uc2e_ref))):
        copies.append(pltpu.make_async_copy(source, target, sems.at[n]))
        copies[n].start()
    probes, points = charges_ref.shape
    local = points // PTS
    lane = lax.broadcasted_iota(i32, (1, PTS), 1)
    sub = lax.broadcasted_iota(i32, (8, PTS), 0)
    first = first_ref[0]
    zero = jnp.zeros((probes, PTS), jnp.bfloat16)
    for copy in copies[:4]:
        copy.wait()
    surface = surface_ref[...]

    leaving = []
    for g in range(0, local, 2):
        parts = []
        for h in (g, g + 1):
            at = slice(h * PTS, (h + 1) * PTS)
            parts.append(split(jnp.where(lane < counts_ref[h], charges_ref[:, at], 0.0)))
        both = slice(g * PTS, (g + 2) * PTS)
        tile_hi, tile_lo = split(surface_tile(offsets_ref[:, both] - 0.5, surface))
        tile_hi_ref[:, both] = tile_hi
        tile_lo_ref[:, both] = tile_lo
        left = jnp.concatenate([parts[0][0], zero], 1), jnp.concatenate([zero, parts[1][0]], 1)
        small = jnp.concatenate([parts[0][1], zero], 1), jnp.concatenate([zero, parts[1][1]], 1)
        large = dot_t(jnp.concatenate(left + small, 0), tile_hi)
        fine = dot_t(jnp.concatenate(left, 0), tile_lo)
        value = (large[:2 * probes] + (large[2 * probes:] + fine)) * inv_four_pi
        gap = jnp.zeros((2 * probes, 2 * PTS - value.shape[1]), f32)
        value = jnp.concatenate([value, gap], 1)
        for half in range(2):
            at = slice(half * PTS, (half + 1) * PTS)
            check_ref[half, pl.ds(g, probes, stride=local), :] = value[:probes, at]
            check_ref[half, pl.ds(g + 1, probes, stride=local), :] = value[probes:, at]
        if (g + 2) % 8 == 0:
            done = slice((g - 6) * PTS, (g + 2) * PTS)
            for source, target in ((tile_hi_ref, tile_hi_hbm), (tile_lo_ref, tile_lo_hbm)):
                leaving.append(pltpu.make_async_copy(source.at[:, done], target.at[:, done], sems.at[5]))
                leaving[-1].start()

    rows = probes * local
    even = lax.rem(lax.div(first, local), 2) == 0
    deep = 8 + probes
    for e in range(GHOST):
        leaf = jnp.where(even, e, local - GHOST + e), jnp.where(even, local - GHOST + e, e)
        for h, ref, skip in ((leaf[0], odd_ref, 0), (leaf[1], pair_ref, rows * 5 // 4)):
            at = pl.multiple_of(h * PTS, PTS)
            corner = [corner_of(first + h, axis) for axis in range(3)]
            held = counts_ref[h]
            xyz = jnp.concatenate([offsets_ref[:, pl.ds(at, PTS)], jnp.zeros((5, PTS), f32)], 0)
            move = jnp.where(sub == 0, corner[0], jnp.where(sub == 1, corner[1], jnp.where(sub == 2, corner[2],
                   jnp.where(sub == 3, held.astype(f32), 0.0))))
            ref[skip + e * deep:skip + e * deep + 8] = xyz + move
            ref[skip + e * deep + 8:skip + (e + 1) * deep] = jnp.where(lane < held, charges_ref[:, pl.ds(at, PTS)], 0.0)

    copies[4].wait()
    up = dot_t3(jnp.concatenate([check_ref[0], check_ref[1]], 1), padded(uc2e_ref, 2 * PTS, 2 * PTS))
    rest = rows // 4
    tail = up[:rest, PTS:]
    for k in range(1, 4):
        tail = tail + pltpu.roll(up[k * rest:(k + 1) * rest, PTS:], 32 * k, 1)
    for target in (up_ref, pair_ref):
        target[:rows] = up[:, :PTS]
        target[rows:rows + rest] = tail
    for copy in leaving:
        copy.wait()


def up_call(first, counts, offsets, charges, uc2e):
    local = counts.shape[0]
    probes, points = charges.shape
    smem = pl.BlockSpec(memory_space=pltpu.SMEM)
    vmem = pl.BlockSpec(memory_space=pltpu.VMEM)
    hbm = pl.BlockSpec(memory_space=pltpu.HBM)
    f32, bf16 = jnp.float32, jnp.bfloat16
    surface = surface_rows()
    sent = probes * local * 5 // 4
    ghost = GHOST * (8 + probes)
    return pl.pallas_call(
        up_kernel,
        out_shape=(
            jax.ShapeDtypeStruct((ghost, PTS), f32),
            jax.ShapeDtypeStruct((sent + ghost, PTS), f32),
            jax.ShapeDtypeStruct((sent, PTS), f32),
            jax.ShapeDtypeStruct((surface.shape[0], points), bf16),
            jax.ShapeDtypeStruct((surface.shape[0], points), bf16),
        ),
        in_specs=[smem, hbm, hbm, hbm, hbm, hbm],
        out_specs=(vmem, vmem, vmem, hbm, hbm),
        scratch_shapes=[
            pltpu.VMEM((surface.shape[0], points), bf16),
            pltpu.VMEM((surface.shape[0], points), bf16),
            pltpu.SMEM(counts.shape, jnp.int32),
            pltpu.VMEM(offsets.shape, f32),
            pltpu.VMEM(charges.shape, f32),
            pltpu.VMEM(uc2e.shape, f32),
            pltpu.VMEM(surface.shape, f32),
            pltpu.VMEM((2, probes * local, PTS), f32),
            pltpu.SemaphoreType.DMA((6,)),
        ],
        compiler_params=pltpu.CompilerParams(vmem_limit_bytes=60 << 20),
        cost_estimate=pl.CostEstimate(flops=500_000_000, bytes_accessed=1_500_000, transcendentals=600_000),
        name="upward",
    )(first, counts, offsets, charges, uc2e, jnp.asarray(surface))


def send_order(count):
    return [count - 1, 1, *range(count - 2, 1, -1), 0]


def far_kernel(counts_ref, wanted_ref, tile_hi_ref, tile_lo_ref, near_ref, vsrc_ref, vtype_ref, m2l_ref, dc2e_ref,
               *refs):
    f32, bf16, i32 = jnp.float32, jnp.bfloat16, jnp.int32
    sent = refs[:-9]
    pieces = [sent[i] for i in np.argsort(send_order(len(sent)))]
    out_ref, code_ref, tally_ref, table_ref, x_hi_ref, x_lo_ref, w_hi_ref, w_lo_ref, eq_ref = refs[-9:]
    probes, points = out_ref.shape
    local = points // PTS
    bits, cap = wanted_ref.shape
    depth = len(pieces) * local
    equiv = m2l_ref.shape[0]
    kinds = m2l_ref.shape[1] // equiv
    rest = equiv - PTS
    rows = probes * local
    lane = lax.broadcasted_iota(i32, (1, PTS), 1)

    w_hi_ref[...] = jnp.zeros_like(w_hi_ref)
    w_lo_ref[...] = jnp.zeros_like(w_lo_ref)
    grown = w_hi_ref.shape[0]
    fill = jnp.zeros((grown - equiv, PTS), f32)
    for t in range(kinds):
        main = jnp.concatenate([m2l_ref[:, t * equiv:t * equiv + PTS], fill], 0)
        w_hi_ref[:, t * PTS:(t + 1) * PTS], w_lo_ref[:, t * PTS:(t + 1) * PTS] = split(main)
    gap = jnp.zeros((equiv, 32 - rest), f32)
    for t in range(0, kinds, 4):
        row = []
        for k in range(4):
            row += [m2l_ref[:, (t + k) * equiv + PTS:(t + k + 1) * equiv], gap]
        tail = jnp.concatenate([jnp.concatenate(row, 1), fill], 0)
        at = kinds * PTS + t * 32
        w_hi_ref[:, at:at + PTS], w_lo_ref[:, at:at + PTS] = split(tail)

    codes = vsrc_ref[...]
    slots = codes.shape[1]
    found = codes - bits * cap + bits * local
    for b in range(bits):
        for s in range(cap):
            found = jnp.where(codes == b * cap + s, b * local + wanted_ref[b, s], found)
    code_ref[...] = jnp.full(code_ref.shape, -1.0, f32)
    code_ref[0:local, 0:slots] = found.astype(f32)
    code_ref[local:, 0:slots] = vtype_ref[...].astype(f32)

    per = PTS // slots
    spot = lax.broadcasted_iota(i32, (8, 8 * slots), 1) // slots == lax.broadcasted_iota(i32, (8, 8 * slots), 0)

    def flat(value):
        wide = jnp.where(lane < slots, value, 0.0)
        total = wide
        for k in range(1, per):
            total = total + pltpu.roll(wide, slots * k, 1)
        total = jnp.concatenate([total] * (8 // per), 1)
        return jnp.sum(jnp.where(spot, total, 0.0), 0, keepdims=True)

    row_id = lax.broadcasted_iota(i32, (8 * kinds, 8 * slots), 0)
    mine = lax.broadcasted_iota(i32, (8 * kinds, 8 * slots), 1) // slots == row_id % 8
    kind = (row_id // 8).astype(f32)
    table_row = lax.broadcasted_iota(i32, (depth, 8 * slots), 0).astype(f32)
    for g in range(0, local, 8):
        take = flat(code_ref[g:g + 8, :])
        sort = flat(code_ref[local + g:local + g + 8, :])
        pick = jnp.where(mine & (sort == kind), 1.0, 0.0).astype(bf16)
        hit = jnp.where(take == table_row, 1.0, 0.0).astype(bf16)
        count = dot_t(pick, hit)
        for t in range(kinds):
            tally_ref[t * local + g:t * local + g + 8, :] = count[8 * t:8 * t + 8]
    tally = tally_ref[...].astype(bf16)

    blocks = probes * 5 // 4
    for b, piece in enumerate(pieces):
        for n in range(blocks):
            hi, lo = split(piece[n * local:(n + 1) * local, :])
            table_ref[b * local:(b + 1) * local, n * PTS:(n + 1) * PTS] = hi
            table_ref[depth + b * local:depth + (b + 1) * local, n * PTS:(n + 1) * PTS] = lo

    twice = jnp.concatenate([tally, tally], 1)
    group = lane // 32
    quarter = probes // 4
    for n in range(0, blocks, 2):
        both = dot(twice, table_ref[:, n * PTS:(n + 2) * PTS])
        for half in range(2):
            q = n + half
            part = both[:, half * PTS:(half + 1) * PTS]
            if q < probes:
                hi, lo = split(part)
                for t in range(kinds):
                    x_hi_ref[q * local:(q + 1) * local, t * PTS:(t + 1) * PTS] = hi[t * local:(t + 1) * local]
                    x_lo_ref[q * local:(q + 1) * local, t * PTS:(t + 1) * PTS] = lo[t * local:(t + 1) * local]
            else:
                for k in range(4):
                    to = (q - probes + quarter * k) * local
                    for t in range(0, kinds, 4):
                        value = jnp.zeros((local, PTS), f32)
                        for i in range(4):
                            moved = part[(t + i) * local:(t + i + 1) * local]
                            if i != k:
                                moved = pltpu.roll(moved, (32 * (i - k)) % PTS, 1)
                            value = jnp.where(group == i, moved, value)
                        at = kinds * PTS + t * 32
                        x_hi_ref[to:to + local, at:at + PTS], x_lo_ref[to:to + local, at:at + PTS] = split(value)

    down = dot_t(x_hi_ref[...], w_hi_ref[...]) + (dot_t(x_hi_ref[...], w_lo_ref[...]) + dot_t(x_lo_ref[...], w_hi_ref[...]))
    equivs = dot_t3(down, padded(dc2e_ref, 2 * PTS, 2 * PTS))
    eq_ref[0], eq_ref[1] = equivs[:, :PTS], equivs[:, PTS:]

    reach = tile_hi_ref.shape[0]
    for g in range(0, local, 2):
        at = slice(g * PTS, (g + 2) * PTS)
        tile_hi, tile_lo = tile_hi_ref[:, at], tile_lo_ref[:, at]
        parts = []
        for h in (g, g + 1):
            value = jnp.concatenate([eq_ref[half, pl.ds(h, probes, stride=local), :] for half in range(2)], 1)[:, :reach]
            parts.append(split(value))
        left = parts[0][0], parts[1][0]
        large = dot(jnp.concatenate(left + (parts[0][1], parts[1][1]), 0), tile_hi)
        value = large[:2 * probes] + (large[2 * probes:] + dot(jnp.concatenate(left, 0), tile_lo))
        for i in range(2):
            h = g + i
            to = slice(h * PTS, (h + 1) * PTS)
            part = value[i * probes:(i + 1) * probes, i * PTS:(i + 1) * PTS] * inv_four_pi
            out_ref[:, to] = jnp.where(lane < counts_ref[h], near_ref[:, to] + part, 0.0)


def far_call(counts, wanted, tiles, near, v_src, v_type, m2l, dc2e, pieces):
    local = counts.shape[0]
    probes, points = near.shape
    equiv = dc2e.shape[0]
    kinds = m2l.shape[1] // equiv
    smem = pl.BlockSpec(memory_space=pltpu.SMEM)
    vmem = pl.BlockSpec(memory_space=pltpu.VMEM)
    f32, bf16 = jnp.float32, jnp.bfloat16
    rows = probes * local
    wide = kinds * (PTS + 32)
    return pl.pallas_call(
        far_kernel,
        out_shape=jax.ShapeDtypeStruct((probes, points), f32),
        in_specs=[smem, smem] + [vmem] * (7 + len(pieces)),
        out_specs=vmem,
        scratch_shapes=[
            pltpu.VMEM((2 * local, PTS), f32),
            pltpu.VMEM((kinds * local, len(pieces) * local), f32),
            pltpu.VMEM((2 * len(pieces) * local, probes * 5 // 4 * PTS), bf16),
            pltpu.VMEM((rows, wide), bf16),
            pltpu.VMEM((rows, wide), bf16),
            pltpu.VMEM((2 * PTS, wide), bf16),
            pltpu.VMEM((2 * PTS, wide), bf16),
            pltpu.VMEM((2, rows, PTS), f32),
        ],
        compiler_params=pltpu.CompilerParams(vmem_limit_bytes=32 << 20),
        cost_estimate=pl.CostEstimate(flops=4_000_000_000, bytes_accessed=4_000_000, transcendentals=600_000),
        name="far",
    )(counts, wanted, *tiles, near, v_src, v_type, m2l, dc2e, *(pieces[i] for i in send_order(len(pieces))))


def shards(offsets, charges, counts, u_list, v_src, v_type, wanted, m2l, uc2e, dc2e):
    local_leaves = counts.shape[0]
    first = (lax.axis_index("cube") * local_leaves).astype(jnp.int32).reshape(1)
    odd, pair, up, tile_hi, tile_lo = up_call(first, counts, offsets, charges, uc2e)
    count = lax.axis_size("cube")
    odd = lax.ppermute(odd, "cube", [(i, i + 1 if i % 2 else i - 1) for i in range(1, count - 1)])
    pieces = [from_partner(up, "cube", bit) for bit in range(count.bit_length() - 2, 0, -1)]
    pair = from_partner(pair, "cube", 0)
    pieces = [pair] + pieces[::-1] + [up]
    near = near_call(first, counts, offsets, charges, pair, odd, u_list)
    return far_call(counts, wanted[0], (tile_hi, tile_lo), near, v_src, v_type, m2l, dc2e, pieces)


def solution(mesh):
    in_specs = (
        P(None, "cube"),
        P(None, "cube"),
        P("cube"),
        P("cube", None),
        P("cube", None),
        P("cube", None),
        P("cube", None, None),
        P(),
        P(),
        P(),
    )
    out_specs = P(None, "cube")
    return jax.shard_map(shards, mesh=mesh, in_specs=in_specs, out_specs=out_specs, check_vma=False)
```

```python
import math

import jax
import jax.numpy as jnp
import numpy as np
from jax import lax
from jax.experimental import pallas as pl
from jax.experimental.pallas import tpu as pltpu
from jax.sharding import PartitionSpec as P

GHOST = 8
PTS = 128
UNIT = 8
UNIT_LOG = 3
SIDE = 3


soften = 0.01
inv_four_pi = 1.0 / (4.0 * math.pi)
surface_radius = 0.55
highest = lax.Precision.HIGHEST


def from_partner(array, axis, bit):
    return lax.ppermute(array, axis, [(i, i ^ 1 << bit) for i in range(lax.axis_size(axis))])


def surface_table():
    lattice = np.arange(6)
    coords = np.stack(np.meshgrid(lattice, lattice, lattice, indexing="ij"), 0).reshape(3, -1)
    coords = (coords - 2.5) / 2.5
    on_face = np.max(np.abs(coords), axis=0) > 0.99
    return coords[:, on_face].astype(np.float32)


def corner_of(leaf, axis):
    summed = jnp.int32(0)
    for digit in range(10):
        summed = summed + (((leaf >> (3 * digit + axis)) & 1) << digit)
    return summed.astype(jnp.float32)


def prepare(m2l_ref, vsrc_ref, vtype_ref, w_hi_ref, w_lo_ref, twice_ref, code_ref, tally_ref):
    f32, bf16, i32 = jnp.float32, jnp.bfloat16, jnp.int32
    local = vsrc_ref.shape[0]
    equiv = m2l_ref.shape[0]
    kinds = m2l_ref.shape[1] // equiv
    depth = twice_ref.shape[1] // 2
    rest = equiv - PTS
    lane = lax.broadcasted_iota(i32, (1, PTS), 1)

    grown = w_hi_ref.shape[0]
    fill = jnp.zeros((grown - equiv, PTS), f32)

    def lanes_from(at, count):
        block, shift = at // PTS, at % PTS
        part = m2l_ref[:, block * PTS:(block + 1) * PTS]
        if shift:
            part = pltpu.roll(part, PTS - shift, 1)
            if shift + count > PTS:
                after = pltpu.roll(m2l_ref[:, (block + 1) * PTS:(block + 2) * PTS], PTS - shift, 1)
                part = jnp.where(lane < PTS - shift, part, after)
        return part

    def tail_from(at, to):
        block, shift = at // PTS, at % PTS
        part = pltpu.roll(m2l_ref[:, block * PTS:(block + 1) * PTS], (to - shift) % PTS, 1)
        if shift + rest > PTS:
            after = pltpu.roll(m2l_ref[:, (block + 1) * PTS:(block + 2) * PTS], (to - shift) % PTS, 1)
            part = jnp.where(lane < to + PTS - shift, part, after)
        return part

    def operators(first):
        for t in range(first, first + 4):
            main = jnp.concatenate([lanes_from(t * equiv, PTS), fill], 0)
            w_hi_ref[:, t * PTS:(t + 1) * PTS], w_lo_ref[:, t * PTS:(t + 1) * PTS] = split(main)
        tail = jnp.zeros((equiv, PTS), f32)
        for k in range(4):
            mine = (lane >= 32 * k) & (lane < 32 * k + rest)
            tail = jnp.where(mine, tail_from((first + k) * equiv + PTS, 32 * k), tail)
        tail = jnp.concatenate([tail, fill], 0)
        at = kinds * PTS + first * 32
        w_hi_ref[:, at:at + PTS], w_lo_ref[:, at:at + PTS] = split(tail)

    for first in range(0, kinds, 4):
        operators(first)
    slots = vsrc_ref.shape[1]
    code_ref[...] = jnp.full(code_ref.shape, -1.0, f32)
    code_ref[0:local, 0:slots] = vsrc_ref[...].astype(f32)
    code_ref[local:, 0:slots] = vtype_ref[...].astype(f32)

    per = PTS // slots
    spot = lax.broadcasted_iota(i32, (8, 8 * slots), 1) // slots == lax.broadcasted_iota(i32, (8, 8 * slots), 0)

    def flat(value):
        wide = jnp.where(lane < slots, value, 0.0)
        total = wide
        for k in range(1, per):
            total = total + pltpu.roll(wide, slots * k, 1)
        total = jnp.concatenate([total] * (8 // per), 1)
        return jnp.sum(jnp.where(spot, total, 0.0), 0, keepdims=True)

    row_id = lax.broadcasted_iota(i32, (8 * kinds, 8 * slots), 0)
    mine = lax.broadcasted_iota(i32, (8 * kinds, 8 * slots), 1) // slots == row_id % 8
    kind = (row_id // 8).astype(f32)
    table_row = lax.broadcasted_iota(i32, (2 * depth, 8 * slots), 0)
    table_row = jnp.where(table_row < depth, table_row, table_row - depth).astype(f32)
    for g in range(0, local, 8):
        take = flat(code_ref[g:g + 8, :])
        sort = flat(code_ref[local + g:local + g + 8, :])
        pick = jnp.where(mine & (sort == kind), 1.0, 0.0).astype(bf16)
        hit = jnp.where(take == table_row, 1.0, 0.0).astype(bf16)
        count = dot_t(pick, hit)
        for t in range(kinds):
            tally_ref[t * local + g:t * local + g + 8, :] = count[8 * t:8 * t + 8]
    twice_ref[...] = tally_ref[...].astype(bf16)


def near_kernel(first_ref, counts_ref, offsets_ref, charges_ref, pair_ref, odd_ref, ulist_ref, m2l_ref, vsrc_ref, vtype_ref,
                out_ref, w_hi_ref, w_lo_ref, twice_ref, code_ref, tally_ref, ghost_ref,
                lanes_ref, chg_ref, src_ref, tgt_ref, square_ref, hi_ref, lo_ref, acc_ref,
                mult_ref, res_ref, start_ref, leaf_ref, from_ref, to_ref, open_ref, shut_ref):
    f32, bf16, i32 = jnp.float32, jnp.bfloat16, jnp.int32
    local = out_ref.shape[1] // PTS
    every = local + 2 * GHOST
    probes = out_ref.shape[0]
    base = GHOST * PTS
    lane = lax.broadcasted_iota(i32, (1, PTS), 1)

    first = first_ref[0]
    centre = []
    for axis in range(3):
        low = high = jnp.int32(0)
        for digit in range(10):
            low = low + (((first >> (3 * digit + axis)) & 1) << digit)
            high = high + ((((first + local - 1) >> (3 * digit + axis)) & 1) << digit)
        centre.append((low + high + 1).astype(f32) * 0.5)
    sub = lax.broadcasted_iota(i32, (8, PTS), 0)
    shift_by = jnp.where(sub == 0, centre[0], jnp.where(sub == 1, centre[1], jnp.where(sub == 2, centre[2], 0.0)))

    def units(n):
        return ((n + UNIT - 1) >> UNIT_LOG) << UNIT_LOG

    deep = 8 + probes
    even = lax.rem(lax.div(first, local), 2) == 0
    skip = pair_ref.shape[0] - GHOST * deep
    odd, pair = odd_ref[...], pair_ref[skip:]
    ghost_ref[0] = jnp.where(even, odd, pair)
    ghost_ref[1] = jnp.where(even, pair, odd)

    def ghost_count(side, e):
        return jnp.max(ghost_ref[side, e * deep + 3:e * deep + 4, :]).astype(i32)

    starts = [None] * (every + 1)
    starts[GHOST] = jnp.int32(base)
    for e in range(GHOST - 1, -1, -1):
        starts[e] = starts[e + 1] - units(ghost_count(0, e))
    for e in range(GHOST, GHOST + local):
        starts[e + 1] = starts[e] + units(counts_ref[e - GHOST])
    for e in range(GHOST + local, every):
        starts[e + 1] = starts[e] + units(ghost_count(1, e - GHOST - local))
    for e in range(every + 1):
        start_ref[e] = starts[e]

    per = PTS // UNIT
    for i in range(per):
        leaf_ref[jnp.maximum((starts[0] >> UNIT_LOG) - per + i, 0)] = 0
    for e in range(every):
        for i in range(per if e < every - 1 else 6 * per):
            leaf_ref[(starts[e] >> UNIT_LOG) + i] = e

    for e in range(GHOST + local - 1, GHOST - 1, -1):
        from_ref[(starts[e + 1] - base - 1) >> 8] = e
        from_ref[(starts[e] - base) >> 8] = e
    for e in range(GHOST, GHOST + local):
        to_ref[(starts[e] - base) >> 8] = e
        to_ref[(starts[e + 1] - base - 1) >> 8] = e

    ids = ulist_ref[...] - (first - GHOST)
    which = lax.broadcasted_iota(i32, (local, every), 1)
    tally = jnp.zeros((local, every), f32)
    for u in range(ids.shape[1]):
        tally = tally + (ids[:, u:u + 1] == which).astype(f32)
    tally = tally.T

    lanes_ref[...] = jnp.zeros_like(lanes_ref)
    for e in range(every):
        if e < GHOST:
            block = ghost_ref[0, e * deep:(e + 1) * deep, :]
        elif e < GHOST + local:
            h = e - GHOST
            at = slice(h * PTS, (h + 1) * PTS)
            corner = [corner_of(first + h, axis) for axis in range(3)]
            move = jnp.where(sub == 0, corner[0], jnp.where(sub == 1, corner[1], corner[2]))
            xyz = jnp.concatenate([offsets_ref[:, at], jnp.zeros((5, PTS), f32)], 0)
            block = jnp.concatenate([xyz + move, jnp.where(lane < counts_ref[h], charges_ref[:, at], 0.0)], 0)
        else:
            at = e - GHOST - local
            block = ghost_ref[1, at * deep:(at + 1) * deep, :]
        block = jnp.concatenate([block[:8] - shift_by, block[8:]], 0)
        shift = starts[e] & (PTS - 1)
        here = pl.multiple_of((starts[e] >> 7) << 7, PTS)
        after = pl.multiple_of(((starts[e] >> 7) + 1) << 7, PTS)
        rolled = pltpu.roll(block, shift, 1)
        keep = lane >= shift
        lanes_ref[:, pl.ds(here, PTS)] = jnp.where(keep, rolled, lanes_ref[:, pl.ds(here, PTS)])
        lanes_ref[:, pl.ds(after, PTS)] = jnp.where(keep, 0.0, rolled)
        if GHOST <= e < GHOST + local:
            col = jnp.broadcast_to(tally[:, e - GHOST:e - GHOST + 1], (every, PTS))
            here = pl.multiple_of(((starts[e] - base) >> 7) * every, 8)
            after = pl.multiple_of((((starts[e] - base) >> 7) + 1) * every, 8)
            mult_ref[pl.ds(here, every), :] = jnp.where(keep, col, mult_ref[pl.ds(here, every), :])
            mult_ref[pl.ds(after, every), :] = col

    prepare(m2l_ref, vsrc_ref, vtype_ref, w_hi_ref, w_lo_ref, twice_ref, code_ref, tally_ref)

    group = 4 * PTS
    head = starts[0] >> 7
    tail = (starts[every] + 127) >> 7
    row_id = lax.broadcasted_iota(i32, (8, group), 0)

    def spread(i, _):
        at = pl.multiple_of((head + 4 * i) * PTS, PTS)
        pos = jnp.where(row_id < 3, lanes_ref[0:8, pl.ds(at, group)], 0.0)
        pos_hi = pos.astype(bf16).astype(f32)
        pos_lo = (pos - pos_hi).astype(bf16).astype(f32)
        used = pos_hi + pos_lo
        norm = jnp.sum(used * used, 0, keepdims=True)

        def rows(blocks, total, three, four):
            parts = []
            for block in blocks[:3]:
                piece = total.astype(bf16).astype(f32)
                total = total - piece
                extra = jnp.where(row_id == three, piece, jnp.where(row_id == four, 1.0, 0.0))
                parts.append(jnp.where(row_id < 3, block, extra))
            return jnp.concatenate(parts + [blocks[3]], 0)

        src = rows((-2.0 * pos_hi, -2.0 * pos_hi, -2.0 * pos_lo, -2.0 * pos_lo), norm + soften, 3, 4)
        tgt = rows((pos_hi, pos_lo, pos_hi, pos_lo), norm, 4, 3)
        src_ref[pl.ds(at, group), :] = src.T.astype(bf16)
        tgt_ref[:, pl.ds(at, group)] = tgt.astype(bf16)
        chg = lanes_ref[8:8 + probes, pl.ds(at, group)]
        hi = chg.astype(bf16)
        chg_ref[0:probes, pl.ds(at, group)] = hi
        chg_ref[probes:2 * probes, pl.ds(at, group)] = (chg - hi.astype(f32)).astype(bf16)
        return 0

    lax.fori_loop(0, (tail - head + 5) // 4, spread, 0)

    acc_ref[...] = jnp.zeros_like(acc_ref)
    blocks = (starts[GHOST + local] - base + 255) >> 8
    steps = jnp.int32(0)
    for t in range(local * PTS // 256 + 1):
        real = t < blocks
        opens = (start_ref[jnp.where(real, from_ref[t], GHOST) - GHOST] >> 7) << 7
        shuts = jnp.where(real, start_ref[jnp.where(real, to_ref[t], GHOST) + GHOST + 1], 0)
        open_ref[t] = opens
        shut_ref[t] = shuts
        steps = steps + jnp.where(real, (shuts - opens + 255) >> 8, 0)

    def advance(step):
        t, row = step
        done = row + 256 >= shut_ref[t]
        after = jnp.minimum(jnp.where(done, t + 1, t), blocks)
        return after, jnp.where(done, open_ref[after], row + 256)

    def square(step, slot):
        t, row = step
        tgt = tgt_ref[:, pl.ds(pl.multiple_of(base + t * 256, 256), 256)]
        square_ref[slot] = jnp.dot(src_ref[pl.ds(pl.multiple_of(row, PTS), 256), :], tgt, preferred_element_type=f32)

    def weigh(step, slot):
        t, row = step
        left = t * (2 * every)
        for r in range(16):
            k = lax.rsqrt(square_ref[slot, 16 * r:16 * r + 16, :])
            parts = []
            for half in range(2):
                leaf = left + leaf_ref[(row >> UNIT_LOG) + 2 * r + half]
                weight = jnp.concatenate([mult_ref[pl.ds(leaf, 1), :], mult_ref[pl.ds(leaf + every, 1), :]], 1)
                parts.append(k[8 * half:8 * half + 8] * weight)
            k = jnp.concatenate(parts, 0)
            at = slice(16 * r, 16 * r + 16)
            hi = k.astype(bf16)
            hi_ref[slot, at, :] = hi
            lo_ref[slot, at, :] = (k - hi.astype(f32)).astype(bf16)

    def gather(step, slot):
        t, row = step
        where = pl.multiple_of(t * 256, 256)
        chg = chg_ref[:, pl.ds(pl.multiple_of(row, PTS), 256)]
        return (where, jnp.dot(chg, hi_ref[slot], preferred_element_type=f32),
                jnp.dot(chg[:probes], lo_ref[slot], preferred_element_type=f32))

    def add(where, first_sum, second_sum):
        acc_ref[0:2 * probes, pl.ds(where, 256)] += first_sum
        acc_ref[2 * probes:, pl.ds(where, 256)] += second_sum

    step = (jnp.int32(0), open_ref[0])
    order = [step]
    for _ in range(2 * SIDE - 1):
        step = advance(step)
        order.append(step)
    for c in range(SIDE):
        square(order[c], c)
    for c in range(SIDE):
        weigh(order[c], c)
    for c in range(SIDE):
        square(order[SIDE + c], c)

    def several(_, order):
        later = []
        step = order[-1]
        for c in range(SIDE):
            step = advance(step)
            later.append(step)
        sums = [gather(order[c], c) for c in range(SIDE)]
        for c in range(SIDE):
            weigh(order[SIDE + c], c)
        for c in range(SIDE):
            square(later[c], c)
        for each in sums:
            add(*each)
        return (*order[SIDE:], *later)

    lax.fori_loop(0, (steps + SIDE - 1) // SIDE, several, tuple(order))
    res_ref[...] = acc_ref[0:probes] + acc_ref[probes:2 * probes] + acc_ref[2 * probes:]

    for g in range(local):
        at = starts[g + GHOST] - base
        shift = at & (PTS - 1)
        here = pl.multiple_of((at >> 7) << 7, PTS)
        after = pl.multiple_of(((at >> 7) + 1) << 7, PTS)
        back = (PTS - shift) & (PTS - 1)
        value = jnp.where(lane < PTS - shift, pltpu.roll(res_ref[:, pl.ds(here, PTS)], back, 1),
                          pltpu.roll(res_ref[:, pl.ds(after, PTS)], back, 1))
        out_ref[:, g * PTS:(g + 1) * PTS] = jnp.where(lane < counts_ref[g], value * inv_four_pi, 0.0)


def near_call(first, counts, offsets, charges, pair, odd, u_list, m2l, v_src, v_type, depth):
    local = counts.shape[0]
    probes = charges.shape[0]
    kinds = m2l.shape[1] // m2l.shape[0]
    every = local + 2 * GHOST
    width = every * PTS + 8 * PTS + 512
    targets = local * PTS + 512
    smem = pl.BlockSpec(memory_space=pltpu.SMEM)
    vmem = pl.BlockSpec(memory_space=pltpu.VMEM)
    return pl.pallas_call(
        near_kernel,
        out_shape=(
            jax.ShapeDtypeStruct((probes, local * PTS), jnp.float32),
            jax.ShapeDtypeStruct((2 * PTS, kinds * (PTS + 32)), jnp.bfloat16),
            jax.ShapeDtypeStruct((2 * PTS, kinds * (PTS + 32)), jnp.bfloat16),
            jax.ShapeDtypeStruct((kinds * local, 2 * depth), jnp.bfloat16),
        ),
        in_specs=[smem, smem] + [vmem] * 8,
        out_specs=(vmem,) * 4,
        scratch_shapes=[
            pltpu.VMEM((2 * local, PTS), jnp.float32),
            pltpu.VMEM((kinds * local, 2 * depth), jnp.float32),
            pltpu.VMEM((2, GHOST * (8 + probes), PTS), jnp.float32),
            pltpu.VMEM((8 + probes, width), jnp.float32),
            pltpu.VMEM((2 * probes, width), jnp.bfloat16),
            pltpu.VMEM((width, 32), jnp.bfloat16),
            pltpu.VMEM((32, width), jnp.bfloat16),
            pltpu.VMEM((SIDE, 256, 256), jnp.float32),
            pltpu.VMEM((SIDE, 256, 256), jnp.bfloat16),
            pltpu.VMEM((SIDE, 256, 256), jnp.bfloat16),
            pltpu.VMEM((3 * probes, targets), jnp.float32),
            pltpu.VMEM((targets // PTS * every, PTS), jnp.float32),
            pltpu.VMEM((probes, targets), jnp.float32),
            pltpu.SMEM((every + 1,), jnp.int32),
            pltpu.SMEM((width // UNIT + 64,), jnp.int32),
            pltpu.SMEM((local * PTS // 256 + 1,), jnp.int32),
            pltpu.SMEM((local * PTS // 256 + 1,), jnp.int32),
            pltpu.SMEM((local * PTS // 256 + 1,), jnp.int32),
            pltpu.SMEM((local * PTS // 256 + 1,), jnp.int32),
        ],
        compiler_params=pltpu.CompilerParams(vmem_limit_bytes=24 << 20),
        cost_estimate=pl.CostEstimate(flops=4_000_000_000, bytes_accessed=2_000_000, transcendentals=4_000_000),
        name="near",
    )(first, counts, offsets, charges, pair, odd, u_list, m2l, v_src, v_type)


def split(value):
    high = value.astype(jnp.bfloat16)
    return high, (value - high.astype(jnp.float32)).astype(jnp.bfloat16)


def dot(left, right):
    return jnp.dot(left, right, preferred_element_type=jnp.float32)


def dot_t(left, right):
    return lax.dot_general(left, right, (((1,), (1,)), ((), ())), preferred_element_type=jnp.float32)


def dot_t3(left, right):
    left_hi, left_lo = split(left)
    right_hi, right_lo = split(right)
    return dot_t(left_hi, right_hi) + (dot_t(left_hi, right_lo) + dot_t(left_lo, right_hi))


def surface_tile(local, surface):
    norm = local[0:1] * local[0:1] + (local[1:2] * local[1:2] + local[2:3] * local[2:3])
    s = (norm + surface[:, 3:4]) + surface[:, 0:1] * local[0:1]
    s = s + (surface[:, 1:2] * local[1:2] + surface[:, 2:3] * local[2:3])
    return lax.rsqrt(s)


def surface_rows():
    points = surface_radius * surface_table().astype(np.float64)
    count = points.shape[1]
    rows = np.zeros((-(-count // 16) * 16, 8), np.float32)
    rows[:count, :3] = -2.0 * points.T
    rows[:count, 3] = (points ** 2).sum(0) + soften
    rows[count:, 3] = 1.0
    return rows


def padded(ref, rows, lanes):
    value = ref[...]
    if value.shape[1] < lanes:
        value = jnp.concatenate([value, jnp.zeros((value.shape[0], lanes - value.shape[1]), value.dtype)], 1)
    if value.shape[0] < rows:
        value = jnp.concatenate([value, jnp.zeros((rows - value.shape[0], lanes), value.dtype)], 0)
    return value


def up_kernel(first_ref, counts_hbm, offsets_hbm, charges_hbm, uc2e_hbm, surface_hbm,
              odd_ref, pair_ref, up_ref, tile_hi_hbm, tile_lo_hbm,
              tile_hi_ref, tile_lo_ref, counts_ref, offsets_ref, charges_ref, uc2e_ref, surface_ref, check_ref, sems):
    f32, i32 = jnp.float32, jnp.int32
    copies = []
    for n, (source, target) in enumerate(((counts_hbm, counts_ref), (offsets_hbm, offsets_ref),
                                          (surface_hbm, surface_ref), (charges_hbm, charges_ref),
                                          (uc2e_hbm, uc2e_ref))):
        copies.append(pltpu.make_async_copy(source, target, sems.at[n]))
        copies[n].start()
    probes, points = charges_ref.shape
    local = points // PTS
    lane = lax.broadcasted_iota(i32, (1, PTS), 1)
    sub = lax.broadcasted_iota(i32, (8, PTS), 0)
    first = first_ref[0]
    zero = jnp.zeros((probes, PTS), jnp.bfloat16)
    for copy in copies[:4]:
        copy.wait()
    surface = surface_ref[...]

    leaving = []
    for g in range(0, local, 2):
        parts = []
        for h in (g, g + 1):
            at = slice(h * PTS, (h + 1) * PTS)
            parts.append(split(jnp.where(lane < counts_ref[h], charges_ref[:, at], 0.0)))
        both = slice(g * PTS, (g + 2) * PTS)
        tile_hi, tile_lo = split(surface_tile(offsets_ref[:, both] - 0.5, surface))
        tile_hi_ref[:, both] = tile_hi
        tile_lo_ref[:, both] = tile_lo
        left = jnp.concatenate([parts[0][0], zero], 1), jnp.concatenate([zero, parts[1][0]], 1)
        small = jnp.concatenate([parts[0][1], zero], 1), jnp.concatenate([zero, parts[1][1]], 1)
        large = dot_t(jnp.concatenate(left + small, 0), tile_hi)
        fine = dot_t(jnp.concatenate(left, 0), tile_lo)
        value = (large[:2 * probes] + (large[2 * probes:] + fine)) * inv_four_pi
        gap = jnp.zeros((2 * probes, 2 * PTS - value.shape[1]), f32)
        value = jnp.concatenate([value, gap], 1)
        for half in range(2):
            at = slice(half * PTS, (half + 1) * PTS)
            check_ref[half, pl.ds(g, probes, stride=local), :] = value[:probes, at]
            check_ref[half, pl.ds(g + 1, probes, stride=local), :] = value[probes:, at]
        if (g + 2) % 8 == 0:
            done = slice((g - 6) * PTS, (g + 2) * PTS)
            for source, target in ((tile_hi_ref, tile_hi_hbm), (tile_lo_ref, tile_lo_hbm)):
                leaving.append(pltpu.make_async_copy(source.at[:, done], target.at[:, done], sems.at[5]))
                leaving[-1].start()

    rows = probes * local
    even = lax.rem(lax.div(first, local), 2) == 0
    deep = 8 + probes
    for e in range(GHOST):
        leaf = jnp.where(even, e, local - GHOST + e), jnp.where(even, local - GHOST + e, e)
        for h, ref, skip in ((leaf[0], odd_ref, 0), (leaf[1], pair_ref, rows * 5 // 4)):
            at = pl.multiple_of(h * PTS, PTS)
            corner = [corner_of(first + h, axis) for axis in range(3)]
            held = counts_ref[h]
            xyz = jnp.concatenate([offsets_ref[:, pl.ds(at, PTS)], jnp.zeros((5, PTS), f32)], 0)
            move = jnp.where(sub == 0, corner[0], jnp.where(sub == 1, corner[1], jnp.where(sub == 2, corner[2],
                   jnp.where(sub == 3, held.astype(f32), 0.0))))
            ref[skip + e * deep:skip + e * deep + 8] = xyz + move
            ref[skip + e * deep + 8:skip + (e + 1) * deep] = jnp.where(lane < held, charges_ref[:, pl.ds(at, PTS)], 0.0)

    copies[4].wait()
    up = dot_t3(jnp.concatenate([check_ref[0], check_ref[1]], 1), padded(uc2e_ref, 2 * PTS, 2 * PTS))
    rest = rows // 4
    tail = up[:rest, PTS:]
    for k in range(1, 4):
        tail = tail + pltpu.roll(up[k * rest:(k + 1) * rest, PTS:], 32 * k, 1)
    for target in (up_ref, pair_ref):
        target[:rows] = up[:, :PTS]
        target[rows:rows + rest] = tail
    for copy in leaving:
        copy.wait()


def up_call(first, counts, offsets, charges, uc2e):
    local = counts.shape[0]
    probes, points = charges.shape
    smem = pl.BlockSpec(memory_space=pltpu.SMEM)
    vmem = pl.BlockSpec(memory_space=pltpu.VMEM)
    hbm = pl.BlockSpec(memory_space=pltpu.HBM)
    f32, bf16 = jnp.float32, jnp.bfloat16
    surface = surface_rows()
    sent = probes * local * 5 // 4
    ghost = GHOST * (8 + probes)
    return pl.pallas_call(
        up_kernel,
        out_shape=(
            jax.ShapeDtypeStruct((ghost, PTS), f32),
            jax.ShapeDtypeStruct((sent + ghost, PTS), f32),
            jax.ShapeDtypeStruct((sent, PTS), f32),
            jax.ShapeDtypeStruct((surface.shape[0], points), bf16),
            jax.ShapeDtypeStruct((surface.shape[0], points), bf16),
        ),
        in_specs=[smem, hbm, hbm, hbm, hbm, hbm],
        out_specs=(vmem, vmem, vmem, hbm, hbm),
        scratch_shapes=[
            pltpu.VMEM((surface.shape[0], points), bf16),
            pltpu.VMEM((surface.shape[0], points), bf16),
            pltpu.SMEM(counts.shape, jnp.int32),
            pltpu.VMEM(offsets.shape, f32),
            pltpu.VMEM(charges.shape, f32),
            pltpu.VMEM(uc2e.shape, f32),
            pltpu.VMEM(surface.shape, f32),
            pltpu.VMEM((2, probes * local, PTS), f32),
            pltpu.SemaphoreType.DMA((6,)),
        ],
        compiler_params=pltpu.CompilerParams(vmem_limit_bytes=60 << 20),
        cost_estimate=pl.CostEstimate(flops=500_000_000, bytes_accessed=1_500_000, transcendentals=600_000),
        name="upward",
    )(first, counts, offsets, charges, uc2e, jnp.asarray(surface))


def send_order(count):
    half = count // 2
    return [count - 1, *range(half, count - 1), *range(half - 1, 0, -1), 0]


def far_kernel(counts_ref, wanted_ref, tile_hi_ref, tile_lo_ref, near_ref, w_hi_ref, w_lo_ref, twice_ref, dc2e_ref,
               *refs):
    f32, bf16, i32 = jnp.float32, jnp.bfloat16, jnp.int32
    sent = refs[:-6]
    pieces = [sent[i] for i in np.argsort(send_order(len(sent)))]
    out_ref, pick_ref, table_ref, x_hi_ref, x_lo_ref, eq_ref = refs[-6:]
    probes, points = out_ref.shape
    local = points // PTS
    bits, cap = wanted_ref.shape
    depth = bits * cap + local
    kinds = w_hi_ref.shape[1] // (PTS + 32)
    twice = twice_ref[...]
    rows = probes * local
    lane = lax.broadcasted_iota(i32, (1, PTS), 1)

    blocks = probes * 5 // 4
    for b in range(bits):
        for c in range(cap):
            pick_ref[pl.ds(b * cap + c, blocks, stride=depth), :] = pieces[b][pl.ds(wanted_ref[b, c], blocks, stride=local), :]
    for n in range(blocks):
        pick_ref[n * depth + bits * cap:(n + 1) * depth, :] = pieces[bits][n * local:(n + 1) * local, :]
    for n in range(blocks):
        hi, lo = split(pick_ref[n * depth:(n + 1) * depth, :])
        table_ref[:depth, n * PTS:(n + 1) * PTS] = hi
        table_ref[depth:, n * PTS:(n + 1) * PTS] = lo

    group = lane // 32
    quarter = probes // 4
    def spread(part, q):
        hi, lo = split(part)
        for t in range(kinds):
            x_hi_ref[q * local:(q + 1) * local, t * PTS:(t + 1) * PTS] = hi[t * local:(t + 1) * local]
            x_lo_ref[q * local:(q + 1) * local, t * PTS:(t + 1) * PTS] = lo[t * local:(t + 1) * local]

    def spread_rest(part, q):
        for t in range(0, kinds, 4):
            kinds4 = [part[(t + i) * local:(t + i + 1) * local] for i in range(4)]

            def mix(pick):
                value = pick(3)
                for i in range(3):
                    value = jnp.where(group == i, pick(i), value)
                return value

            moved = []
            for shift in range(4):
                value = mix(lambda k: kinds4[(k + shift) % 4])
                moved.append(pltpu.roll(value, 32 * shift, 1) if shift else value)
            at = kinds * PTS + t * 32
            for k in range(4):
                to = (q + quarter * k) * local
                value = mix(lambda i: moved[(i - k) % 4])
                x_hi_ref[to:to + local, at:at + PTS], x_lo_ref[to:to + local, at:at + PTS] = split(value)

    for n in range(0, probes, 2):
        both = dot(twice, table_ref[:, n * PTS:(n + 2) * PTS])
        spread(both[:, :PTS], n)
        spread(both[:, PTS:], n + 1)

    def down_part(at):
        x_hi, x_lo, w_hi, w_lo = x_hi_ref[:, at], x_lo_ref[:, at], w_hi_ref[:, at], w_lo_ref[:, at]
        return dot_t(jnp.concatenate([x_hi, x_hi, x_lo], 1), jnp.concatenate([w_hi, w_lo, w_hi], 1))

    down = None
    for c in range(kinds // 4):
        value = down_part(slice(4 * c * PTS, 4 * (c + 1) * PTS))
        down = value if down is None else down + value
        for q in range(c, quarter, kinds // 4):
            spread_rest(dot(twice, table_ref[:, (probes + q) * PTS:(probes + q + 1) * PTS]), q)
    down = down + down_part(slice(kinds * PTS, kinds * (PTS + 32)))
    equivs = dot_t3(down, padded(dc2e_ref, 2 * PTS, 2 * PTS))
    eq_ref[0], eq_ref[1] = equivs[:, :PTS], equivs[:, PTS:]

    reach = tile_hi_ref.shape[0]
    for g in range(0, local, 2):
        at = slice(g * PTS, (g + 2) * PTS)
        tile_hi, tile_lo = tile_hi_ref[:, at], tile_lo_ref[:, at]
        parts = []
        for h in (g, g + 1):
            value = jnp.concatenate([eq_ref[half, pl.ds(h, probes, stride=local), :] for half in range(2)], 1)[:, :reach]
            parts.append(split(value))
        left = parts[0][0], parts[1][0]
        large = dot(jnp.concatenate(left + (parts[0][1], parts[1][1]), 0), tile_hi)
        value = large[:2 * probes] + (large[2 * probes:] + dot(jnp.concatenate(left, 0), tile_lo))
        for i in range(2):
            h = g + i
            to = slice(h * PTS, (h + 1) * PTS)
            part = value[i * probes:(i + 1) * probes, i * PTS:(i + 1) * PTS] * inv_four_pi
            out_ref[:, to] = jnp.where(lane < counts_ref[h], near_ref[:, to] + part, 0.0)


def far_call(counts, wanted, tiles, near, w_hi, w_lo, twice, dc2e, pieces):
    local = counts.shape[0]
    probes, points = near.shape
    kinds = w_hi.shape[1] // (PTS + 32)
    smem = pl.BlockSpec(memory_space=pltpu.SMEM)
    vmem = pl.BlockSpec(memory_space=pltpu.VMEM)
    f32, bf16 = jnp.float32, jnp.bfloat16
    rows = probes * local
    wide = kinds * (PTS + 32)
    depth = wanted.shape[0] * wanted.shape[1] + local
    return pl.pallas_call(
        far_kernel,
        out_shape=jax.ShapeDtypeStruct((probes, points), f32),
        in_specs=[smem, smem] + [vmem] * (7 + len(pieces)),
        out_specs=vmem,
        scratch_shapes=[
            pltpu.VMEM((probes * 5 // 4 * depth, PTS), f32),
            pltpu.VMEM((2 * depth, probes * 5 // 4 * PTS), bf16),
            pltpu.VMEM((rows, wide), bf16),
            pltpu.VMEM((rows, wide), bf16),
            pltpu.VMEM((2, rows, PTS), f32),
        ],
        compiler_params=pltpu.CompilerParams(vmem_limit_bytes=32 << 20),
        cost_estimate=pl.CostEstimate(flops=4_000_000_000, bytes_accessed=4_000_000, transcendentals=600_000),
        name="far",
    )(counts, wanted, *tiles, near, w_hi, w_lo, twice, dc2e, *(pieces[i] for i in send_order(len(pieces))))


def shards(offsets, charges, counts, u_list, v_src, v_type, wanted, m2l, uc2e, dc2e):
    local_leaves = counts.shape[0]
    first = (lax.axis_index("cube") * local_leaves).astype(jnp.int32).reshape(1)
    odd, pair, up, tile_hi, tile_lo = up_call(first, counts, offsets, charges, uc2e)
    count = lax.axis_size("cube")
    odd = lax.ppermute(odd, "cube", [(i, i + 1 if i % 2 else i - 1) for i in range(1, count - 1)])
    pieces = [from_partner(up, "cube", bit) for bit in range(count.bit_length() - 2, 0, -1)]
    pair = from_partner(pair, "cube", 0)
    pieces = [pair] + pieces[::-1] + [up]
    depth = wanted.shape[1] * wanted.shape[2] + counts.shape[0]
    near, w_hi, w_lo, twice = near_call(first, counts, offsets, charges, pair, odd, u_list, m2l, v_src, v_type, depth)
    return far_call(counts, wanted[0], (tile_hi, tile_lo), near, w_hi, w_lo, twice, dc2e, pieces)


def solution(mesh):
    in_specs = (
        P(None, "cube"),
        P(None, "cube"),
        P("cube"),
        P("cube", None),
        P("cube", None),
        P("cube", None),
        P("cube", None, None),
        P(),
        P(),
        P(),
    )
    out_specs = P(None, "cube")
    return jax.shard_map(shards, mesh=mesh, in_specs=in_specs, out_specs=out_specs, check_vma=False)
```

```python
import math

import jax
import jax.numpy as jnp
import numpy as np
from jax import lax
from jax.experimental import pallas as pl
from jax.experimental.pallas import tpu as pltpu
from jax.sharding import PartitionSpec as P

GHOST = 8
PTS = 128
UNIT = 8
UNIT_LOG = 3
SIDE = 3


soften = 0.01
inv_four_pi = 1.0 / (4.0 * math.pi)
surface_radius = 0.55
highest = lax.Precision.HIGHEST


def from_partner(array, axis, bit):
    return lax.ppermute(array, axis, [(i, i ^ 1 << bit) for i in range(lax.axis_size(axis))])


def surface_table():
    lattice = np.arange(6)
    coords = np.stack(np.meshgrid(lattice, lattice, lattice, indexing="ij"), 0).reshape(3, -1)
    coords = (coords - 2.5) / 2.5
    on_face = np.max(np.abs(coords), axis=0) > 0.99
    return coords[:, on_face].astype(np.float32)


def corner_of(leaf, axis):
    summed = jnp.int32(0)
    for digit in range(10):
        summed = summed + (((leaf >> (3 * digit + axis)) & 1) << digit)
    return summed.astype(jnp.float32)


def corners(first, local):
    base = [corner_of(first, axis) for axis in range(3)]

    def at(h, axis):
        if local & (local - 1):
            return corner_of(first + h, axis)
        return base[axis] + float(sum(((h >> (3 * digit + axis)) & 1) << digit for digit in range(10)))

    return at


def prepare(m2l_ref, vsrc_ref, vtype_ref, w_hi_ref, w_lo_ref, twice_ref, code_ref, tally_ref):
    f32, bf16, i32 = jnp.float32, jnp.bfloat16, jnp.int32
    local = vsrc_ref.shape[0]
    equiv = m2l_ref.shape[0]
    kinds = m2l_ref.shape[1] // equiv
    depth = twice_ref.shape[1] // 2
    rest = equiv - PTS
    lane = lax.broadcasted_iota(i32, (1, PTS), 1)

    grown = w_hi_ref.shape[0]
    fill = jnp.zeros((grown - equiv, PTS), f32)

    def lanes_from(at, count):
        block, shift = at // PTS, at % PTS
        part = m2l_ref[:, block * PTS:(block + 1) * PTS]
        if shift:
            part = pltpu.roll(part, PTS - shift, 1)
            if shift + count > PTS:
                after = pltpu.roll(m2l_ref[:, (block + 1) * PTS:(block + 2) * PTS], PTS - shift, 1)
                part = jnp.where(lane < PTS - shift, part, after)
        return part

    def tail_from(at, to):
        block, shift = at // PTS, at % PTS
        part = pltpu.roll(m2l_ref[:, block * PTS:(block + 1) * PTS], (to - shift) % PTS, 1)
        if shift + rest > PTS:
            after = pltpu.roll(m2l_ref[:, (block + 1) * PTS:(block + 2) * PTS], (to - shift) % PTS, 1)
            part = jnp.where(lane < to + PTS - shift, part, after)
        return part

    def operators(first):
        for t in range(first, first + 4):
            main = jnp.concatenate([lanes_from(t * equiv, PTS), fill], 0)
            w_hi_ref[:, t * PTS:(t + 1) * PTS], w_lo_ref[:, t * PTS:(t + 1) * PTS] = split(main)
        tail = jnp.zeros((equiv, PTS), f32)
        for k in range(4):
            mine = (lane >= 32 * k) & (lane < 32 * k + rest)
            tail = jnp.where(mine, tail_from((first + k) * equiv + PTS, 32 * k), tail)
        tail = jnp.concatenate([tail, fill], 0)
        at = kinds * PTS + first * 32
        w_hi_ref[:, at:at + PTS], w_lo_ref[:, at:at + PTS] = split(tail)

    for first in range(0, kinds, 4):
        operators(first)
    slots = vsrc_ref.shape[1]
    code_ref[...] = jnp.full(code_ref.shape, -1.0, f32)
    code_ref[0:local, 0:slots] = vsrc_ref[...].astype(f32)
    code_ref[local:, 0:slots] = vtype_ref[...].astype(f32)

    per = PTS // slots
    spot = lax.broadcasted_iota(i32, (8, 8 * slots), 1) // slots == lax.broadcasted_iota(i32, (8, 8 * slots), 0)

    def flat(value):
        wide = jnp.where(lane < slots, value, 0.0)
        total = wide
        for k in range(1, per):
            total = total + pltpu.roll(wide, slots * k, 1)
        total = jnp.concatenate([total] * (8 // per), 1)
        return jnp.sum(jnp.where(spot, total, 0.0), 0, keepdims=True)

    row_id = lax.broadcasted_iota(i32, (8 * kinds, 8 * slots), 0)
    mine = lax.broadcasted_iota(i32, (8 * kinds, 8 * slots), 1) // slots == row_id % 8
    kind = (row_id // 8).astype(f32)
    table_row = lax.broadcasted_iota(i32, (2 * depth, 8 * slots), 0)
    table_row = jnp.where(table_row < depth, table_row, table_row - depth).astype(f32)
    for g in range(0, local, 8):
        take = flat(code_ref[g:g + 8, :])
        sort = flat(code_ref[local + g:local + g + 8, :])
        pick = jnp.where(mine & (sort == kind), 1.0, 0.0).astype(bf16)
        hit = jnp.where(take == table_row, 1.0, 0.0).astype(bf16)
        count = dot_t(pick, hit)
        for t in range(kinds):
            tally_ref[t * local + g:t * local + g + 8, :] = count[8 * t:8 * t + 8]
    twice_ref[...] = tally_ref[...].astype(bf16)


def near_kernel(first_ref, counts_ref, offsets_ref, charges_ref, pair_ref, odd_ref, ulist_ref, m2l_ref, vsrc_ref, vtype_ref,
                surface_ref, out_ref, w_hi_ref, w_lo_ref, twice_ref, tile_hi_ref, tile_lo_ref, code_ref, tally_ref, ghost_ref,
                lanes_ref, chg_ref, src_ref, tgt_ref, square_ref, hi_ref, lo_ref, acc_ref,
                mult_ref, res_ref, start_ref, leaf_ref, from_ref, to_ref, open_ref, shut_ref):
    f32, bf16, i32 = jnp.float32, jnp.bfloat16, jnp.int32
    local = out_ref.shape[1] // PTS
    every = local + 2 * GHOST
    probes = out_ref.shape[0]
    base = GHOST * PTS
    lane = lax.broadcasted_iota(i32, (1, PTS), 1)

    first = first_ref[0]
    corner_at = corners(first, local)
    centre = [(corner_at(0, axis) + corner_at(local - 1, axis) + 1.0) * 0.5 for axis in range(3)]
    sub = lax.broadcasted_iota(i32, (8, PTS), 0)
    shift_by = jnp.where(sub == 0, centre[0], jnp.where(sub == 1, centre[1], jnp.where(sub == 2, centre[2], 0.0)))

    def units(n):
        return ((n + UNIT - 1) >> UNIT_LOG) << UNIT_LOG

    deep = 8 + probes
    even = lax.rem(lax.div(first, local), 2) == 0
    skip = pair_ref.shape[0] - GHOST * deep
    odd, pair = odd_ref[...], pair_ref[skip:]
    ghost_ref[0] = jnp.where(even, odd, pair)
    ghost_ref[1] = jnp.where(even, pair, odd)

    def ghost_count(side, e):
        return jnp.max(ghost_ref[side, e * deep + 3:e * deep + 4, :]).astype(i32)

    starts = [None] * (every + 1)
    starts[GHOST] = jnp.int32(base)
    for e in range(GHOST - 1, -1, -1):
        starts[e] = starts[e + 1] - units(ghost_count(0, e))
    for e in range(GHOST, GHOST + local):
        starts[e + 1] = starts[e] + units(counts_ref[e - GHOST])
    for e in range(GHOST + local, every):
        starts[e + 1] = starts[e] + units(ghost_count(1, e - GHOST - local))
    for e in range(every + 1):
        start_ref[e] = starts[e]

    per = PTS // UNIT
    for i in range(per):
        leaf_ref[jnp.maximum((starts[0] >> UNIT_LOG) - per + i, 0)] = 0
    for e in range(every):
        for i in range(per if e < every - 1 else 6 * per):
            leaf_ref[(starts[e] >> UNIT_LOG) + i] = e

    for e in range(GHOST + local - 1, GHOST - 1, -1):
        from_ref[(starts[e + 1] - base - 1) >> 8] = e
        from_ref[(starts[e] - base) >> 8] = e
    for e in range(GHOST, GHOST + local):
        to_ref[(starts[e] - base) >> 8] = e
        to_ref[(starts[e + 1] - base - 1) >> 8] = e

    ids = ulist_ref[...] - (first - GHOST)
    which = lax.broadcasted_iota(i32, (local, every), 1)
    tally = jnp.zeros((local, every), f32)
    for u in range(ids.shape[1]):
        tally = tally + (ids[:, u:u + 1] == which).astype(f32)
    tally = tally.T

    lanes_ref[...] = jnp.zeros_like(lanes_ref)
    for e in range(every):
        if e < GHOST:
            block = ghost_ref[0, e * deep:(e + 1) * deep, :]
        elif e < GHOST + local:
            h = e - GHOST
            at = slice(h * PTS, (h + 1) * PTS)
            corner = [corner_at(h, axis) for axis in range(3)]
            move = jnp.where(sub == 0, corner[0], jnp.where(sub == 1, corner[1], corner[2]))
            xyz = jnp.concatenate([offsets_ref[:, at], jnp.zeros((5, PTS), f32)], 0)
            block = jnp.concatenate([xyz + move, jnp.where(lane < counts_ref[h], charges_ref[:, at], 0.0)], 0)
        else:
            at = e - GHOST - local
            block = ghost_ref[1, at * deep:(at + 1) * deep, :]
        block = jnp.concatenate([block[:8] - shift_by, block[8:]], 0)
        shift = starts[e] & (PTS - 1)
        here = pl.multiple_of((starts[e] >> 7) << 7, PTS)
        after = pl.multiple_of(((starts[e] >> 7) + 1) << 7, PTS)
        rolled = pltpu.roll(block, shift, 1)
        keep = lane >= shift
        lanes_ref[:, pl.ds(here, PTS)] = jnp.where(keep, rolled, lanes_ref[:, pl.ds(here, PTS)])
        lanes_ref[:, pl.ds(after, PTS)] = jnp.where(keep, 0.0, rolled)
        if GHOST <= e < GHOST + local:
            col = jnp.broadcast_to(tally[:, e - GHOST:e - GHOST + 1], (every, PTS))
            here = pl.multiple_of(((starts[e] - base) >> 7) * every, 8)
            after = pl.multiple_of((((starts[e] - base) >> 7) + 1) * every, 8)
            mult_ref[pl.ds(here, every), :] = jnp.where(keep, col, mult_ref[pl.ds(here, every), :])
            mult_ref[pl.ds(after, every), :] = col

    prepare(m2l_ref, vsrc_ref, vtype_ref, w_hi_ref, w_lo_ref, twice_ref, code_ref, tally_ref)

    group = 4 * PTS
    head = starts[0] >> 7
    tail = (starts[every] + 127) >> 7
    row_id = lax.broadcasted_iota(i32, (8, group), 0)

    def spread(i, _):
        at = pl.multiple_of((head + 4 * i) * PTS, PTS)
        pos = jnp.where(row_id < 3, lanes_ref[0:8, pl.ds(at, group)], 0.0)
        pos_hi = pos.astype(bf16).astype(f32)
        pos_lo = (pos - pos_hi).astype(bf16).astype(f32)
        used = pos_hi + pos_lo
        norm = jnp.sum(used * used, 0, keepdims=True)

        def rows(blocks, total, three, four):
            parts = []
            for block in blocks[:3]:
                piece = total.astype(bf16).astype(f32)
                total = total - piece
                extra = jnp.where(row_id == three, piece, jnp.where(row_id == four, 1.0, 0.0))
                parts.append(jnp.where(row_id < 3, block, extra))
            return jnp.concatenate(parts + [blocks[3]], 0)

        src = rows((-2.0 * pos_hi, -2.0 * pos_hi, -2.0 * pos_lo, -2.0 * pos_lo), norm + soften, 3, 4)
        tgt = rows((pos_hi, pos_lo, pos_hi, pos_lo), norm, 4, 3)
        src_ref[pl.ds(at, group), :] = src.T.astype(bf16)
        tgt_ref[:, pl.ds(at, group)] = tgt.astype(bf16)
        chg = lanes_ref[8:8 + probes, pl.ds(at, group)]
        hi = chg.astype(bf16)
        chg_ref[0:probes, pl.ds(at, group)] = hi
        chg_ref[probes:2 * probes, pl.ds(at, group)] = (chg - hi.astype(f32)).astype(bf16)
        return 0

    lax.fori_loop(0, (tail - head + 5) // 4, spread, 0)

    acc_ref[...] = jnp.zeros_like(acc_ref)
    blocks = (starts[GHOST + local] - base + 255) >> 8
    steps = jnp.int32(0)
    for t in range(local * PTS // 256 + 1):
        real = t < blocks
        opens = (start_ref[jnp.where(real, from_ref[t], GHOST) - GHOST] >> 7) << 7
        shuts = jnp.where(real, start_ref[jnp.where(real, to_ref[t], GHOST) + GHOST + 1], 0)
        open_ref[t] = opens
        shut_ref[t] = shuts
        steps = steps + jnp.where(real, (shuts - opens + 255) >> 8, 0)

    def advance(step):
        t, row = step
        done = row + 256 >= shut_ref[t]
        after = jnp.minimum(jnp.where(done, t + 1, t), blocks)
        return after, jnp.where(done, open_ref[after], row + 256)

    def square(step, slot):
        t, row = step
        tgt = tgt_ref[:, pl.ds(pl.multiple_of(base + t * 256, 256), 256)]
        square_ref[slot] = jnp.dot(src_ref[pl.ds(pl.multiple_of(row, PTS), 256), :], tgt, preferred_element_type=f32)

    def weigh(step, slot):
        t, row = step
        left = t * (2 * every)
        for r in range(16):
            k = lax.rsqrt(square_ref[slot, 16 * r:16 * r + 16, :])
            parts = []
            for half in range(2):
                leaf = left + leaf_ref[(row >> UNIT_LOG) + 2 * r + half]
                weight = jnp.concatenate([mult_ref[pl.ds(leaf, 1), :], mult_ref[pl.ds(leaf + every, 1), :]], 1)
                parts.append(k[8 * half:8 * half + 8] * weight)
            k = jnp.concatenate(parts, 0)
            at = slice(16 * r, 16 * r + 16)
            hi = k.astype(bf16)
            hi_ref[slot, at, :] = hi
            lo_ref[slot, at, :] = (k - hi.astype(f32)).astype(bf16)

    def gather(step, slot):
        t, row = step
        where = pl.multiple_of(t * 256, 256)
        chg = chg_ref[:, pl.ds(pl.multiple_of(row, PTS), 256)]
        return (where, jnp.dot(chg, hi_ref[slot], preferred_element_type=f32),
                jnp.dot(chg[:probes], lo_ref[slot], preferred_element_type=f32))

    def add(where, first_sum, second_sum):
        acc_ref[0:2 * probes, pl.ds(where, 256)] += first_sum
        acc_ref[2 * probes:, pl.ds(where, 256)] += second_sum

    step = (jnp.int32(0), open_ref[0])
    order = [step]
    for _ in range(2 * SIDE - 1):
        step = advance(step)
        order.append(step)
    for c in range(SIDE):
        square(order[c], c)
    for c in range(SIDE):
        weigh(order[c], c)
    for c in range(SIDE):
        square(order[SIDE + c], c)

    def several(_, order):
        later = []
        step = order[-1]
        for c in range(SIDE):
            step = advance(step)
            later.append(step)
        sums = [gather(order[c], c) for c in range(SIDE)]
        for c in range(SIDE):
            weigh(order[SIDE + c], c)
        for c in range(SIDE):
            square(later[c], c)
        for each in sums:
            add(*each)
        return (*order[SIDE:], *later)

    lax.fori_loop(0, (steps + SIDE - 1) // SIDE, several, tuple(order))
    res_ref[...] = acc_ref[0:probes] + acc_ref[probes:2 * probes] + acc_ref[2 * probes:]

    def tile(i, _):
        for half in range(2):
            at = pl.ds(pl.multiple_of((2 * i + half) * PTS, PTS), PTS)
            x = offsets_ref[:, at] - 0.5
            norm = x[0:1] * x[0:1] + (x[1:2] * x[1:2] + x[2:3] * x[2:3])
            for r in range(0, tile_hi_ref.shape[0], 16):
                rows = slice(r, r + 16)
                s = (surface_ref[3, rows, :] + norm) + surface_ref[0, rows, :] * x[0:1]
                s = s + (surface_ref[1, rows, :] * x[1:2] + surface_ref[2, rows, :] * x[2:3])
                tile_hi_ref[rows, at], tile_lo_ref[rows, at] = split(lax.rsqrt(s))
        return 0

    lax.fori_loop(0, local // 2, tile, 0, unroll=2)

    for g in range(local):
        at = starts[g + GHOST] - base
        shift = at & (PTS - 1)
        here = pl.multiple_of((at >> 7) << 7, PTS)
        after = pl.multiple_of(((at >> 7) + 1) << 7, PTS)
        back = (PTS - shift) & (PTS - 1)
        value = jnp.where(lane < PTS - shift, pltpu.roll(res_ref[:, pl.ds(here, PTS)], back, 1),
                          pltpu.roll(res_ref[:, pl.ds(after, PTS)], back, 1))
        out_ref[:, g * PTS:(g + 1) * PTS] = jnp.where(lane < counts_ref[g], value * inv_four_pi, 0.0)


def near_call(first, counts, offsets, charges, pair, odd, u_list, m2l, v_src, v_type, depth):
    local = counts.shape[0]
    probes = charges.shape[0]
    kinds = m2l.shape[1] // m2l.shape[0]
    spread = np.ascontiguousarray(np.broadcast_to(surface_rows().T[:4, :, None], (4, surface_rows().shape[0], PTS)))
    grown = -(-m2l.shape[0] // 16) * 16
    every = local + 2 * GHOST
    width = every * PTS + 8 * PTS + 512
    targets = local * PTS + 512
    smem = pl.BlockSpec(memory_space=pltpu.SMEM)
    vmem = pl.BlockSpec(memory_space=pltpu.VMEM)
    return pl.pallas_call(
        near_kernel,
        out_shape=(
            jax.ShapeDtypeStruct((probes, local * PTS), jnp.float32),
            jax.ShapeDtypeStruct((grown, kinds * (PTS + 32)), jnp.bfloat16),
            jax.ShapeDtypeStruct((grown, kinds * (PTS + 32)), jnp.bfloat16),
            jax.ShapeDtypeStruct((kinds * local, 2 * depth), jnp.bfloat16),
            jax.ShapeDtypeStruct((spread.shape[1], local * PTS), jnp.bfloat16),
            jax.ShapeDtypeStruct((spread.shape[1], local * PTS), jnp.bfloat16),
        ),
        in_specs=[smem, smem] + [vmem] * 9,
        out_specs=(vmem,) * 6,
        scratch_shapes=[
            pltpu.VMEM((2 * local, PTS), jnp.float32),
            pltpu.VMEM((kinds * local, 2 * depth), jnp.float32),
            pltpu.VMEM((2, GHOST * (8 + probes), PTS), jnp.float32),
            pltpu.VMEM((8 + probes, width), jnp.float32),
            pltpu.VMEM((2 * probes, width), jnp.bfloat16),
            pltpu.VMEM((width, 32), jnp.bfloat16),
            pltpu.VMEM((32, width), jnp.bfloat16),
            pltpu.VMEM((SIDE, 256, 256), jnp.float32),
            pltpu.VMEM((SIDE, 256, 256), jnp.bfloat16),
            pltpu.VMEM((SIDE, 256, 256), jnp.bfloat16),
            pltpu.VMEM((3 * probes, targets), jnp.float32),
            pltpu.VMEM((targets // PTS * every, PTS), jnp.float32),
            pltpu.VMEM((probes, targets), jnp.float32),
            pltpu.SMEM((every + 1,), jnp.int32),
            pltpu.SMEM((width // UNIT + 64,), jnp.int32),
            pltpu.SMEM((local * PTS // 256 + 1,), jnp.int32),
            pltpu.SMEM((local * PTS // 256 + 1,), jnp.int32),
            pltpu.SMEM((local * PTS // 256 + 1,), jnp.int32),
            pltpu.SMEM((local * PTS // 256 + 1,), jnp.int32),
        ],
        compiler_params=pltpu.CompilerParams(vmem_limit_bytes=24 << 20),
        cost_estimate=pl.CostEstimate(flops=4_000_000_000, bytes_accessed=2_000_000, transcendentals=4_000_000),
        name="near",
    )(first, counts, offsets, charges, pair, odd, u_list, m2l, v_src, v_type, jnp.asarray(spread))


def split(value):
    high = value.astype(jnp.bfloat16)
    return high, (value - high.astype(jnp.float32)).astype(jnp.bfloat16)


def dot(left, right):
    return jnp.dot(left, right, preferred_element_type=jnp.float32)


def dot_t(left, right):
    return lax.dot_general(left, right, (((1,), (1,)), ((), ())), preferred_element_type=jnp.float32)


def dot_t3(left, right):
    left_hi, left_lo = split(left)
    right_hi, right_lo = split(right)
    return dot_t(left_hi, right_hi) + (dot_t(left_hi, right_lo) + dot_t(left_lo, right_hi))


def surface_tile(local, surface):
    norm = local[0:1] * local[0:1] + (local[1:2] * local[1:2] + local[2:3] * local[2:3])
    s = (norm + surface[:, 3:4]) + surface[:, 0:1] * local[0:1]
    s = s + (surface[:, 1:2] * local[1:2] + surface[:, 2:3] * local[2:3])
    return lax.rsqrt(s)


def surface_rows():
    points = surface_radius * surface_table().astype(np.float64)
    count = points.shape[1]
    rows = np.zeros((-(-count // 16) * 16, 8), np.float32)
    rows[:count, :3] = -2.0 * points.T
    rows[:count, 3] = (points ** 2).sum(0) + soften
    rows[count:, 3] = 1.0
    return rows


def padded(ref, rows, lanes):
    value = ref[...]
    if value.shape[1] < lanes:
        value = jnp.concatenate([value, jnp.zeros((value.shape[0], lanes - value.shape[1]), value.dtype)], 1)
    if value.shape[0] < rows:
        value = jnp.concatenate([value, jnp.zeros((rows - value.shape[0], lanes), value.dtype)], 0)
    return value


def up_kernel(first_ref, counts_hbm, offsets_hbm, charges_hbm, uc2e_hbm, surface_hbm,
              odd_ref, pair_ref, up_ref, counts_ref, offsets_ref, charges_ref, uc2e_ref, surface_ref, check_ref, sems):
    f32, i32 = jnp.float32, jnp.int32
    copies = []
    for n, (source, target) in enumerate(((counts_hbm, counts_ref), (offsets_hbm, offsets_ref),
                                          (surface_hbm, surface_ref), (charges_hbm, charges_ref),
                                          (uc2e_hbm, uc2e_ref))):
        copies.append(pltpu.make_async_copy(source, target, sems.at[n]))
        copies[n].start()
    probes, points = charges_ref.shape
    local = points // PTS
    lane = lax.broadcasted_iota(i32, (1, PTS), 1)
    sub = lax.broadcasted_iota(i32, (8, PTS), 0)
    first = first_ref[0]
    zero = jnp.zeros((probes, PTS), jnp.bfloat16)
    for copy in copies[:4]:
        copy.wait()
    surface = surface_ref[...]

    for g in range(0, local, 2):
        parts = []
        for h in (g, g + 1):
            at = slice(h * PTS, (h + 1) * PTS)
            parts.append(split(jnp.where(lane < counts_ref[h], charges_ref[:, at], 0.0)))
        both = slice(g * PTS, (g + 2) * PTS)
        tile_hi, tile_lo = split(surface_tile(offsets_ref[:, both] - 0.5, surface))
        left = jnp.concatenate([parts[0][0], zero], 1), jnp.concatenate([zero, parts[1][0]], 1)
        small = jnp.concatenate([parts[0][1], zero], 1), jnp.concatenate([zero, parts[1][1]], 1)
        large = dot_t(jnp.concatenate(left + small, 0), tile_hi)
        fine = dot_t(jnp.concatenate(left, 0), tile_lo)
        value = (large[:2 * probes] + (large[2 * probes:] + fine)) * inv_four_pi
        gap = jnp.zeros((2 * probes, 2 * PTS - value.shape[1]), f32)
        value = jnp.concatenate([value, gap], 1)
        for half in range(2):
            at = slice(half * PTS, (half + 1) * PTS)
            check_ref[half, pl.ds(g, probes, stride=local), :] = value[:probes, at]
            check_ref[half, pl.ds(g + 1, probes, stride=local), :] = value[probes:, at]

    rows = probes * local
    even = lax.rem(lax.div(first, local), 2) == 0
    corner_at = corners(first, local)
    deep = 8 + probes
    for e in range(GHOST):
        ends = e, local - GHOST + e
        for ids, ref, skip in ((ends, odd_ref, 0), (ends[::-1], pair_ref, rows * 5 // 4)):
            h = jnp.where(even, *ids)
            at = pl.multiple_of(h * PTS, PTS)
            corner = [jnp.where(even, corner_at(ids[0], axis), corner_at(ids[1], axis)) for axis in range(3)]
            held = counts_ref[h]
            xyz = jnp.concatenate([offsets_ref[:, pl.ds(at, PTS)], jnp.zeros((5, PTS), f32)], 0)
            move = jnp.where(sub == 0, corner[0], jnp.where(sub == 1, corner[1], jnp.where(sub == 2, corner[2],
                   jnp.where(sub == 3, held.astype(f32), 0.0))))
            ref[skip + e * deep:skip + e * deep + 8] = xyz + move
            ref[skip + e * deep + 8:skip + (e + 1) * deep] = jnp.where(lane < held, charges_ref[:, pl.ds(at, PTS)], 0.0)

    copies[4].wait()
    up = dot_t3(jnp.concatenate([check_ref[0], check_ref[1]], 1), padded(uc2e_ref, 2 * PTS, 2 * PTS))
    rest = rows // 4
    tail = up[:rest, PTS:]
    for k in range(1, 4):
        tail = tail + pltpu.roll(up[k * rest:(k + 1) * rest, PTS:], 32 * k, 1)
    for target in (up_ref, pair_ref):
        target[:rows] = up[:, :PTS]
        target[rows:rows + rest] = tail


def up_call(first, counts, offsets, charges, uc2e):
    local = counts.shape[0]
    probes = charges.shape[0]
    smem = pl.BlockSpec(memory_space=pltpu.SMEM)
    vmem = pl.BlockSpec(memory_space=pltpu.VMEM)
    hbm = pl.BlockSpec(memory_space=pltpu.HBM)
    f32 = jnp.float32
    surface = surface_rows()
    sent = probes * local * 5 // 4
    ghost = GHOST * (8 + probes)
    return pl.pallas_call(
        up_kernel,
        out_shape=(
            jax.ShapeDtypeStruct((ghost, PTS), f32),
            jax.ShapeDtypeStruct((sent + ghost, PTS), f32),
            jax.ShapeDtypeStruct((sent, PTS), f32),
        ),
        in_specs=[smem, hbm, hbm, hbm, hbm, hbm],
        out_specs=(vmem,) * 3,
        scratch_shapes=[
            pltpu.SMEM(counts.shape, jnp.int32),
            pltpu.VMEM(offsets.shape, f32),
            pltpu.VMEM(charges.shape, f32),
            pltpu.VMEM(uc2e.shape, f32),
            pltpu.VMEM(surface.shape, f32),
            pltpu.VMEM((2, probes * local, PTS), f32),
            pltpu.SemaphoreType.DMA((5,)),
        ],
        compiler_params=pltpu.CompilerParams(vmem_limit_bytes=60 << 20),
        cost_estimate=pl.CostEstimate(flops=500_000_000, bytes_accessed=1_500_000, transcendentals=600_000),
        name="upward",
    )(first, counts, offsets, charges, uc2e, jnp.asarray(surface))


def send_order(count):
    half = count // 2
    return [count - 1, *range(half, count - 1), *range(half - 1, 0, -1), 0]


def far_kernel(counts_ref, wanted_ref, tile_hi_ref, tile_lo_ref, near_ref, w_hi_ref, w_lo_ref, twice_ref, dc2e_ref,
               *refs):
    f32, bf16, i32 = jnp.float32, jnp.bfloat16, jnp.int32
    sent = refs[:-7]
    pieces = [sent[i] for i in np.argsort(send_order(len(sent)))]
    out_ref, pick_ref, table_ref, x_hi_ref, x_lo_ref, eq_ref, down_ref = refs[-7:]
    probes, points = out_ref.shape
    local = points // PTS
    bits, cap = wanted_ref.shape
    depth = bits * cap + local
    kinds = w_hi_ref.shape[1] // (PTS + 32)
    twice = twice_ref[...]
    rows = probes * local
    lane = lax.broadcasted_iota(i32, (1, PTS), 1)

    blocks = probes * 5 // 4
    for b in range(bits):
        for c in range(cap):
            pick_ref[pl.ds(b * cap + c, blocks, stride=depth), :] = pieces[b][pl.ds(wanted_ref[b, c], blocks, stride=local), :]
    for n in range(blocks):
        pick_ref[n * depth + bits * cap:(n + 1) * depth, :] = pieces[bits][n * local:(n + 1) * local, :]
    for n in range(blocks):
        hi, lo = split(pick_ref[n * depth:(n + 1) * depth, :])
        table_ref[:depth, n * PTS:(n + 1) * PTS] = hi
        table_ref[depth:, n * PTS:(n + 1) * PTS] = lo

    group = lane // 32
    quarter = probes // 4
    def spread(part, q):
        hi, lo = split(part)
        for t in range(kinds):
            x_hi_ref[q * local:(q + 1) * local, t * PTS:(t + 1) * PTS] = hi[t * local:(t + 1) * local]
            x_lo_ref[q * local:(q + 1) * local, t * PTS:(t + 1) * PTS] = lo[t * local:(t + 1) * local]

    def spread_rest(part, q):
        for t in range(0, kinds, 4):
            kinds4 = [part[(t + i) * local:(t + i + 1) * local] for i in range(4)]

            def mix(pick):
                value = pick(3)
                for i in range(3):
                    value = jnp.where(group == i, pick(i), value)
                return value

            moved = []
            for shift in range(4):
                value = mix(lambda k: kinds4[(k + shift) % 4])
                moved.append(pltpu.roll(value, 32 * shift, 1) if shift else value)
            at = kinds * PTS + t * 32
            for k in range(4):
                to = (q + quarter * k) * local
                value = mix(lambda i: moved[(i - k) % 4])
                x_hi_ref[to:to + local, at:at + PTS], x_lo_ref[to:to + local, at:at + PTS] = split(value)

    for n in range(0, probes, 2):
        both = dot(twice, table_ref[:, n * PTS:(n + 2) * PTS])
        spread(both[:, :PTS], n)
        spread(both[:, PTS:], n + 1)

    def down_part(at):
        x_hi, x_lo, w_hi, w_lo = x_hi_ref[:, at], x_lo_ref[:, at], w_hi_ref[:, at], w_lo_ref[:, at]
        return dot_t(jnp.concatenate([x_hi, x_hi, x_lo], 1), jnp.concatenate([w_hi, w_lo, w_hi], 1))

    for q in range(quarter):
        spread_rest(dot(twice, table_ref[:, (probes + q) * PTS:(probes + q + 1) * PTS]), q)

    def add_part(i, _):
        down_ref[...] += down_part(pl.ds(pl.multiple_of(i * cut, PTS), cut))
        return 0

    cut = kinds * (PTS + 32) // 2
    down_ref[...] = jnp.zeros_like(down_ref)
    lax.fori_loop(0, 2, add_part, 0)
    down = down_ref[...]
    equivs = dot_t3(down, padded(dc2e_ref, 2 * PTS, down.shape[1]))
    eq_ref[0], eq_ref[1] = equivs[:, :PTS], equivs[:, PTS:]

    reach = tile_hi_ref.shape[0]
    for g in range(0, local, 2):
        at = slice(g * PTS, (g + 2) * PTS)
        tile_hi, tile_lo = tile_hi_ref[:, at], tile_lo_ref[:, at]
        parts = []
        for h in (g, g + 1):
            value = jnp.concatenate([eq_ref[half, pl.ds(h, probes, stride=local), :] for half in range(2)], 1)[:, :reach]
            parts.append(split(value))
        left = parts[0][0], parts[1][0]
        large = dot(jnp.concatenate(left + (parts[0][1], parts[1][1]), 0), tile_hi)
        value = large[:2 * probes] + (large[2 * probes:] + dot(jnp.concatenate(left, 0), tile_lo))
        for i in range(2):
            h = g + i
            to = slice(h * PTS, (h + 1) * PTS)
            part = value[i * probes:(i + 1) * probes, i * PTS:(i + 1) * PTS] * inv_four_pi
            out_ref[:, to] = jnp.where(lane < counts_ref[h], near_ref[:, to] + part, 0.0)


def far_call(counts, wanted, tiles, near, w_hi, w_lo, twice, dc2e, pieces):
    local = counts.shape[0]
    probes, points = near.shape
    kinds = w_hi.shape[1] // (PTS + 32)
    smem = pl.BlockSpec(memory_space=pltpu.SMEM)
    vmem = pl.BlockSpec(memory_space=pltpu.VMEM)
    f32, bf16 = jnp.float32, jnp.bfloat16
    rows = probes * local
    wide = kinds * (PTS + 32)
    depth = wanted.shape[0] * wanted.shape[1] + local
    return pl.pallas_call(
        far_kernel,
        out_shape=jax.ShapeDtypeStruct((probes, points), f32),
        in_specs=[smem, smem] + [vmem] * (7 + len(pieces)),
        out_specs=vmem,
        scratch_shapes=[
            pltpu.VMEM((probes * 5 // 4 * depth, PTS), f32),
            pltpu.VMEM((2 * depth, probes * 5 // 4 * PTS), bf16),
            pltpu.VMEM((rows, wide), bf16),
            pltpu.VMEM((rows, wide), bf16),
            pltpu.VMEM((2, rows, PTS), f32),
            pltpu.VMEM((rows, w_hi.shape[0]), f32),
        ],
        compiler_params=pltpu.CompilerParams(vmem_limit_bytes=32 << 20),
        cost_estimate=pl.CostEstimate(flops=4_000_000_000, bytes_accessed=4_000_000, transcendentals=600_000),
        name="far",
    )(counts, wanted, *tiles, near, w_hi, w_lo, twice, dc2e, *(pieces[i] for i in send_order(len(pieces))))


def shards(offsets, charges, counts, u_list, v_src, v_type, wanted, m2l, uc2e, dc2e):
    local_leaves = counts.shape[0]
    first = (lax.axis_index("cube") * local_leaves).astype(jnp.int32).reshape(1)
    odd, pair, up = up_call(first, counts, offsets, charges, uc2e)
    count = lax.axis_size("cube")
    odd = lax.ppermute(odd, "cube", [(i, i + 1 if i % 2 else i - 1) for i in range(1, count - 1)])
    pieces = [from_partner(up, "cube", bit) for bit in range(count.bit_length() - 2, 0, -1)]
    pair = from_partner(pair, "cube", 0)
    pieces = [pair] + pieces[::-1] + [up]
    depth = wanted.shape[1] * wanted.shape[2] + counts.shape[0]
    near, w_hi, w_lo, twice, *tiles = near_call(first, counts, offsets, charges, pair, odd, u_list, m2l, v_src, v_type, depth)
    return far_call(counts, wanted[0], tiles, near, w_hi, w_lo, twice, dc2e, pieces)


def solution(mesh):
    in_specs = (
        P(None, "cube"),
        P(None, "cube"),
        P("cube"),
        P("cube", None),
        P("cube", None),
        P("cube", None),
        P("cube", None, None),
        P(),
        P(),
        P(),
    )
    out_specs = P(None, "cube")
    return jax.shard_map(shards, mesh=mesh, in_specs=in_specs, out_specs=out_specs, check_vma=False)
```

```python
import math

import jax
import jax.numpy as jnp
import numpy as np
from jax import lax
from jax.experimental import pallas as pl
from jax.experimental.pallas import tpu as pltpu
from jax.sharding import PartitionSpec as P

GHOST = 8
PTS = 128
UNIT = 8
UNIT_LOG = 3
SIDE = 3


soften = 0.01
inv_four_pi = 1.0 / (4.0 * math.pi)
surface_radius = 0.55
highest = lax.Precision.HIGHEST


def from_partner(array, axis, bit):
    return lax.ppermute(array, axis, [(i, i ^ 1 << bit) for i in range(lax.axis_size(axis))])


def surface_table():
    lattice = np.arange(6)
    coords = np.stack(np.meshgrid(lattice, lattice, lattice, indexing="ij"), 0).reshape(3, -1)
    coords = (coords - 2.5) / 2.5
    on_face = np.max(np.abs(coords), axis=0) > 0.99
    return coords[:, on_face].astype(np.float32)


def corner_of(leaf, axis):
    summed = jnp.int32(0)
    for digit in range(10):
        summed = summed + (((leaf >> (3 * digit + axis)) & 1) << digit)
    return summed.astype(jnp.float32)


def corners(first, local):
    base = [corner_of(first, axis) for axis in range(3)]

    def at(h, axis):
        if local & (local - 1):
            return corner_of(first + h, axis)
        return base[axis] + float(sum(((h >> (3 * digit + axis)) & 1) << digit for digit in range(10)))

    return at


def prepare(m2l_ref, vsrc_ref, vtype_ref, w_hi_ref, w_lo_ref, twice_ref, code_ref, tally_ref):
    f32, bf16, i32 = jnp.float32, jnp.bfloat16, jnp.int32
    local = vsrc_ref.shape[0]
    equiv = m2l_ref.shape[0]
    kinds = m2l_ref.shape[1] // equiv
    depth = twice_ref.shape[1] // 2
    rest = equiv - PTS
    lane = lax.broadcasted_iota(i32, (1, PTS), 1)

    grown = w_hi_ref.shape[0]
    fill = jnp.zeros((grown - equiv, PTS), f32)

    def lanes_from(at, count):
        block, shift = at // PTS, at % PTS
        part = m2l_ref[:, block * PTS:(block + 1) * PTS]
        if shift:
            part = pltpu.roll(part, PTS - shift, 1)
            if shift + count > PTS:
                after = pltpu.roll(m2l_ref[:, (block + 1) * PTS:(block + 2) * PTS], PTS - shift, 1)
                part = jnp.where(lane < PTS - shift, part, after)
        return part

    def tail_from(at, to):
        block, shift = at // PTS, at % PTS
        part = pltpu.roll(m2l_ref[:, block * PTS:(block + 1) * PTS], (to - shift) % PTS, 1)
        if shift + rest > PTS:
            after = pltpu.roll(m2l_ref[:, (block + 1) * PTS:(block + 2) * PTS], (to - shift) % PTS, 1)
            part = jnp.where(lane < to + PTS - shift, part, after)
        return part

    def operators(first):
        for t in range(first, first + 4):
            main = jnp.concatenate([lanes_from(t * equiv, PTS), fill], 0)
            w_hi_ref[:, t * PTS:(t + 1) * PTS], w_lo_ref[:, t * PTS:(t + 1) * PTS] = split(main)
        tail = jnp.zeros((equiv, PTS), f32)
        for k in range(4):
            mine = (lane >= 32 * k) & (lane < 32 * k + rest)
            tail = jnp.where(mine, tail_from((first + k) * equiv + PTS, 32 * k), tail)
        tail = jnp.concatenate([tail, fill], 0)
        at = kinds * PTS + first * 32
        w_hi_ref[:, at:at + PTS], w_lo_ref[:, at:at + PTS] = split(tail)

    for first in range(0, kinds, 4):
        operators(first)
    slots = vsrc_ref.shape[1]
    code_ref[...] = jnp.full(code_ref.shape, -1.0, f32)
    code_ref[0:local, 0:slots] = vsrc_ref[...].astype(f32)
    code_ref[local:, 0:slots] = vtype_ref[...].astype(f32)

    per = PTS // slots
    spot = lax.broadcasted_iota(i32, (8, 8 * slots), 1) // slots == lax.broadcasted_iota(i32, (8, 8 * slots), 0)

    def flat(value):
        wide = jnp.where(lane < slots, value, 0.0)
        total = wide
        for k in range(1, per):
            total = total + pltpu.roll(wide, slots * k, 1)
        total = jnp.concatenate([total] * (8 // per), 1)
        return jnp.sum(jnp.where(spot, total, 0.0), 0, keepdims=True)

    row_id = lax.broadcasted_iota(i32, (8 * kinds, 8 * slots), 0)
    mine = lax.broadcasted_iota(i32, (8 * kinds, 8 * slots), 1) // slots == row_id % 8
    kind = (row_id // 8).astype(f32)
    table_row = lax.broadcasted_iota(i32, (2 * depth, 8 * slots), 0)
    table_row = jnp.where(table_row < depth, table_row, table_row - depth).astype(f32)
    for g in range(0, local, 8):
        take = flat(code_ref[g:g + 8, :])
        sort = flat(code_ref[local + g:local + g + 8, :])
        pick = jnp.where(mine & (sort == kind), 1.0, 0.0).astype(bf16)
        hit = jnp.where(take == table_row, 1.0, 0.0).astype(bf16)
        count = dot_t(pick, hit)
        for t in range(kinds):
            tally_ref[t * local + g:t * local + g + 8, :] = count[8 * t:8 * t + 8]
    twice_ref[...] = tally_ref[...].astype(bf16)


def near_kernel(first_ref, counts_ref, offsets_ref, charges_ref, pair_ref, odd_ref, ulist_ref, m2l_ref, vsrc_ref, vtype_ref,
                surface_ref, out_ref, w_hi_ref, w_lo_ref, twice_ref, tile_hi_ref, tile_lo_ref, code_ref, tally_ref, ghost_ref,
                lanes_ref, chg_ref, src_ref, tgt_ref, square_ref, hi_ref, lo_ref, acc_ref,
                mult_ref, res_ref, start_ref, leaf_ref, from_ref, to_ref, open_ref, shut_ref):
    f32, bf16, i32 = jnp.float32, jnp.bfloat16, jnp.int32
    local = out_ref.shape[1] // PTS
    every = local + 2 * GHOST
    probes = out_ref.shape[0]
    base = GHOST * PTS
    lane = lax.broadcasted_iota(i32, (1, PTS), 1)

    first = first_ref[0]
    corner_at = corners(first, local)
    centre = [(corner_at(0, axis) + corner_at(local - 1, axis) + 1.0) * 0.5 for axis in range(3)]
    sub = lax.broadcasted_iota(i32, (8, PTS), 0)
    shift_by = jnp.where(sub == 0, centre[0], jnp.where(sub == 1, centre[1], jnp.where(sub == 2, centre[2], 0.0)))

    def units(n):
        return ((n + UNIT - 1) >> UNIT_LOG) << UNIT_LOG

    deep = 8 + probes
    even = lax.rem(lax.div(first, local), 2) == 0
    skip = pair_ref.shape[0] - GHOST * deep
    odd, pair = odd_ref[...], pair_ref[skip:]
    ghost_ref[0] = jnp.where(even, odd, pair)
    ghost_ref[1] = jnp.where(even, pair, odd)

    def ghost_count(side, e):
        return jnp.max(ghost_ref[side, e * deep + 3:e * deep + 4, :]).astype(i32)

    starts = [None] * (every + 1)
    starts[GHOST] = jnp.int32(base)
    for e in range(GHOST - 1, -1, -1):
        starts[e] = starts[e + 1] - units(ghost_count(0, e))
    for e in range(GHOST, GHOST + local):
        starts[e + 1] = starts[e] + units(counts_ref[e - GHOST])
    for e in range(GHOST + local, every):
        starts[e + 1] = starts[e] + units(ghost_count(1, e - GHOST - local))
    for e in range(every + 1):
        start_ref[e] = starts[e]

    per = PTS // UNIT
    for i in range(per):
        leaf_ref[jnp.maximum((starts[0] >> UNIT_LOG) - per + i, 0)] = 0
    for e in range(every):
        for i in range(per if e < every - 1 else 6 * per):
            leaf_ref[(starts[e] >> UNIT_LOG) + i] = e

    for e in range(GHOST + local - 1, GHOST - 1, -1):
        from_ref[(starts[e + 1] - base - 1) >> 8] = e
        from_ref[(starts[e] - base) >> 8] = e
    for e in range(GHOST, GHOST + local):
        to_ref[(starts[e] - base) >> 8] = e
        to_ref[(starts[e + 1] - base - 1) >> 8] = e

    ids = ulist_ref[...] - (first - GHOST)
    which = lax.broadcasted_iota(i32, (local, every), 1)
    tally = jnp.zeros((local, every), f32)
    for u in range(ids.shape[1]):
        tally = tally + (ids[:, u:u + 1] == which).astype(f32)
    tally = tally.T

    lanes_ref[...] = jnp.zeros_like(lanes_ref)
    for e in range(every):
        if e < GHOST:
            block = ghost_ref[0, e * deep:(e + 1) * deep, :]
        elif e < GHOST + local:
            h = e - GHOST
            at = slice(h * PTS, (h + 1) * PTS)
            corner = [corner_at(h, axis) for axis in range(3)]
            move = jnp.where(sub == 0, corner[0], jnp.where(sub == 1, corner[1], corner[2]))
            xyz = jnp.concatenate([offsets_ref[:, at], jnp.zeros((5, PTS), f32)], 0)
            block = jnp.concatenate([xyz + move, jnp.where(lane < counts_ref[h], charges_ref[:, at], 0.0)], 0)
        else:
            at = e - GHOST - local
            block = ghost_ref[1, at * deep:(at + 1) * deep, :]
        block = jnp.concatenate([block[:8] - shift_by, block[8:]], 0)
        shift = starts[e] & (PTS - 1)
        here = pl.multiple_of((starts[e] >> 7) << 7, PTS)
        after = pl.multiple_of(((starts[e] >> 7) + 1) << 7, PTS)
        rolled = pltpu.roll(block, shift, 1)
        keep = lane >= shift
        lanes_ref[:, pl.ds(here, PTS)] = jnp.where(keep, rolled, lanes_ref[:, pl.ds(here, PTS)])
        lanes_ref[:, pl.ds(after, PTS)] = jnp.where(keep, 0.0, rolled)
        if GHOST <= e < GHOST + local:
            col = jnp.broadcast_to(tally[:, e - GHOST:e - GHOST + 1], (every, PTS))
            here = pl.multiple_of(((starts[e] - base) >> 7) * every, 8)
            after = pl.multiple_of((((starts[e] - base) >> 7) + 1) * every, 8)
            mult_ref[pl.ds(here, every), :] = jnp.where(keep, col, mult_ref[pl.ds(here, every), :])
            mult_ref[pl.ds(after, every), :] = col

    prepare(m2l_ref, vsrc_ref, vtype_ref, w_hi_ref, w_lo_ref, twice_ref, code_ref, tally_ref)

    group = 4 * PTS
    head = starts[0] >> 7
    tail = (starts[every] + 127) >> 7
    row_id = lax.broadcasted_iota(i32, (8, group), 0)

    def spread(i, _):
        at = pl.multiple_of((head + 4 * i) * PTS, PTS)
        pos = jnp.where(row_id < 3, lanes_ref[0:8, pl.ds(at, group)], 0.0)
        pos_hi = pos.astype(bf16).astype(f32)
        pos_lo = (pos - pos_hi).astype(bf16).astype(f32)
        used = pos_hi + pos_lo
        norm = jnp.sum(used * used, 0, keepdims=True)

        def rows(blocks, total, three, four):
            parts = []
            for block in blocks[:3]:
                piece = total.astype(bf16).astype(f32)
                total = total - piece
                extra = jnp.where(row_id == three, piece, jnp.where(row_id == four, 1.0, 0.0))
                parts.append(jnp.where(row_id < 3, block, extra))
            return jnp.concatenate(parts + [blocks[3]], 0)

        src = rows((-2.0 * pos_hi, -2.0 * pos_hi, -2.0 * pos_lo, -2.0 * pos_lo), norm + soften, 3, 4)
        tgt = rows((pos_hi, pos_lo, pos_hi, pos_lo), norm, 4, 3)
        src_ref[pl.ds(at, group), :] = src.T.astype(bf16)
        tgt_ref[:, pl.ds(at, group)] = tgt.astype(bf16)
        chg = lanes_ref[8:8 + probes, pl.ds(at, group)]
        hi = chg.astype(bf16)
        chg_ref[0:probes, pl.ds(at, group)] = hi
        chg_ref[probes:2 * probes, pl.ds(at, group)] = (chg - hi.astype(f32)).astype(bf16)
        return 0

    lax.fori_loop(0, (tail - head + 5) // 4, spread, 0)

    acc_ref[...] = jnp.zeros_like(acc_ref)
    blocks = (starts[GHOST + local] - base + 255) >> 8
    steps = jnp.int32(0)
    for t in range(local * PTS // 256 + 1):
        real = t < blocks
        opens = (start_ref[jnp.where(real, from_ref[t], GHOST) - GHOST] >> 7) << 7
        shuts = jnp.where(real, start_ref[jnp.where(real, to_ref[t], GHOST) + GHOST + 1], 0)
        open_ref[t] = opens
        shut_ref[t] = shuts
        steps = steps + jnp.where(real, (shuts - opens + 255) >> 8, 0)

    def advance(step):
        t, row = step
        done = row + 256 >= shut_ref[t]
        after = jnp.minimum(jnp.where(done, t + 1, t), blocks)
        return after, jnp.where(done, open_ref[after], row + 256)

    def square(step, slot):
        t, row = step
        tgt = tgt_ref[:, pl.ds(pl.multiple_of(base + t * 256, 256), 256)]
        square_ref[slot] = jnp.dot(src_ref[pl.ds(pl.multiple_of(row, PTS), 256), :], tgt, preferred_element_type=f32)

    def weigh(step, slot):
        t, row = step
        left = t * (2 * every)
        for r in range(16):
            k = lax.rsqrt(square_ref[slot, 16 * r:16 * r + 16, :])
            parts = []
            for half in range(2):
                leaf = left + leaf_ref[(row >> UNIT_LOG) + 2 * r + half]
                weight = jnp.concatenate([mult_ref[pl.ds(leaf, 1), :], mult_ref[pl.ds(leaf + every, 1), :]], 1)
                parts.append(k[8 * half:8 * half + 8] * weight)
            k = jnp.concatenate(parts, 0)
            at = slice(16 * r, 16 * r + 16)
            hi = k.astype(bf16)
            hi_ref[slot, at, :] = hi
            lo_ref[slot, at, :] = (k - hi.astype(f32)).astype(bf16)

    def gather(step, slot):
        t, row = step
        where = pl.multiple_of(t * 256, 256)
        chg = chg_ref[:, pl.ds(pl.multiple_of(row, PTS), 256)]
        return (where, jnp.dot(chg, hi_ref[slot], preferred_element_type=f32),
                jnp.dot(chg[:probes], lo_ref[slot], preferred_element_type=f32))

    def add(where, first_sum, second_sum):
        acc_ref[0:2 * probes, pl.ds(where, 256)] += first_sum
        acc_ref[2 * probes:, pl.ds(where, 256)] += second_sum

    step = (jnp.int32(0), open_ref[0])
    order = [step]
    for _ in range(2 * SIDE - 1):
        step = advance(step)
        order.append(step)
    for c in range(SIDE):
        square(order[c], c)
    for c in range(SIDE):
        weigh(order[c], c)
    for c in range(SIDE):
        square(order[SIDE + c], c)

    def several(_, order):
        later = []
        step = order[-1]
        for c in range(SIDE):
            step = advance(step)
            later.append(step)
        sums = [gather(order[c], c) for c in range(SIDE)]
        for c in range(SIDE):
            weigh(order[SIDE + c], c)
        for c in range(SIDE):
            square(later[c], c)
        for each in sums:
            add(*each)
        return (*order[SIDE:], *later)

    lax.fori_loop(0, (steps + SIDE - 1) // SIDE, several, tuple(order))
    res_ref[...] = acc_ref[0:probes] + acc_ref[probes:2 * probes] + acc_ref[2 * probes:]

    def tile(i, _):
        for half in range(2):
            at = pl.ds(pl.multiple_of((2 * i + half) * PTS, PTS), PTS)
            x = offsets_ref[:, at] - 0.5
            norm = x[0:1] * x[0:1] + (x[1:2] * x[1:2] + x[2:3] * x[2:3])
            for r in range(0, tile_hi_ref.shape[0], 16):
                rows = slice(r, r + 16)
                s = (surface_ref[3, rows, :] + norm) + surface_ref[0, rows, :] * x[0:1]
                s = s + (surface_ref[1, rows, :] * x[1:2] + surface_ref[2, rows, :] * x[2:3])
                tile_hi_ref[rows, at], tile_lo_ref[rows, at] = split(lax.rsqrt(s))
        return 0

    lax.fori_loop(0, local // 2, tile, 0, unroll=True)

    for g in range(local):
        at = starts[g + GHOST] - base
        shift = at & (PTS - 1)
        here = pl.multiple_of((at >> 7) << 7, PTS)
        after = pl.multiple_of(((at >> 7) + 1) << 7, PTS)
        back = (PTS - shift) & (PTS - 1)
        value = jnp.where(lane < PTS - shift, pltpu.roll(res_ref[:, pl.ds(here, PTS)], back, 1),
                          pltpu.roll(res_ref[:, pl.ds(after, PTS)], back, 1))
        out_ref[:, g * PTS:(g + 1) * PTS] = jnp.where(lane < counts_ref[g], value * inv_four_pi, 0.0)


def near_call(first, counts, offsets, charges, pair, odd, u_list, m2l, v_src, v_type, depth):
    local = counts.shape[0]
    probes = charges.shape[0]
    kinds = m2l.shape[1] // m2l.shape[0]
    spread = np.ascontiguousarray(np.broadcast_to(surface_rows().T[:4, :, None], (4, surface_rows().shape[0], PTS)))
    grown = -(-m2l.shape[0] // 16) * 16
    every = local + 2 * GHOST
    width = every * PTS + 8 * PTS + 512
    targets = local * PTS + 512
    smem = pl.BlockSpec(memory_space=pltpu.SMEM)
    vmem = pl.BlockSpec(memory_space=pltpu.VMEM)
    return pl.pallas_call(
        near_kernel,
        out_shape=(
            jax.ShapeDtypeStruct((probes, local * PTS), jnp.float32),
            jax.ShapeDtypeStruct((grown, kinds * (PTS + 32)), jnp.bfloat16),
            jax.ShapeDtypeStruct((grown, kinds * (PTS + 32)), jnp.bfloat16),
            jax.ShapeDtypeStruct((kinds * local, 2 * depth), jnp.bfloat16),
            jax.ShapeDtypeStruct((spread.shape[1], local * PTS), jnp.bfloat16),
            jax.ShapeDtypeStruct((spread.shape[1], local * PTS), jnp.bfloat16),
        ),
        in_specs=[smem, smem] + [vmem] * 9,
        out_specs=(vmem,) * 6,
        scratch_shapes=[
            pltpu.VMEM((2 * local, PTS), jnp.float32),
            pltpu.VMEM((kinds * local, 2 * depth), jnp.float32),
            pltpu.VMEM((2, GHOST * (8 + probes), PTS), jnp.float32),
            pltpu.VMEM((8 + probes, width), jnp.float32),
            pltpu.VMEM((2 * probes, width), jnp.bfloat16),
            pltpu.VMEM((width, 32), jnp.bfloat16),
            pltpu.VMEM((32, width), jnp.bfloat16),
            pltpu.VMEM((SIDE, 256, 256), jnp.float32),
            pltpu.VMEM((SIDE, 256, 256), jnp.bfloat16),
            pltpu.VMEM((SIDE, 256, 256), jnp.bfloat16),
            pltpu.VMEM((3 * probes, targets), jnp.float32),
            pltpu.VMEM((targets // PTS * every, PTS), jnp.float32),
            pltpu.VMEM((probes, targets), jnp.float32),
            pltpu.SMEM((every + 1,), jnp.int32),
            pltpu.SMEM((width // UNIT + 64,), jnp.int32),
            pltpu.SMEM((local * PTS // 256 + 1,), jnp.int32),
            pltpu.SMEM((local * PTS // 256 + 1,), jnp.int32),
            pltpu.SMEM((local * PTS // 256 + 1,), jnp.int32),
            pltpu.SMEM((local * PTS // 256 + 1,), jnp.int32),
        ],
        compiler_params=pltpu.CompilerParams(vmem_limit_bytes=24 << 20),
        cost_estimate=pl.CostEstimate(flops=4_000_000_000, bytes_accessed=2_000_000, transcendentals=4_000_000),
        name="near",
    )(first, counts, offsets, charges, pair, odd, u_list, m2l, v_src, v_type, jnp.asarray(spread))


def split(value):
    high = value.astype(jnp.bfloat16)
    return high, (value - high.astype(jnp.float32)).astype(jnp.bfloat16)


def dot(left, right):
    return jnp.dot(left, right, preferred_element_type=jnp.float32)


def dot_t(left, right):
    return lax.dot_general(left, right, (((1,), (1,)), ((), ())), preferred_element_type=jnp.float32)


def dot_t3(left, right):
    left_hi, left_lo = split(left)
    right_hi, right_lo = split(right)
    return dot_t(left_hi, right_hi) + (dot_t(left_hi, right_lo) + dot_t(left_lo, right_hi))


def surface_tile(local, surface):
    norm = local[0:1] * local[0:1] + (local[1:2] * local[1:2] + local[2:3] * local[2:3])
    s = (norm + surface[:, 3:4]) + surface[:, 0:1] * local[0:1]
    s = s + (surface[:, 1:2] * local[1:2] + surface[:, 2:3] * local[2:3])
    return lax.rsqrt(s)


def surface_rows():
    points = surface_radius * surface_table().astype(np.float64)
    count = points.shape[1]
    rows = np.zeros((-(-count // 16) * 16, 8), np.float32)
    rows[:count, :3] = -2.0 * points.T
    rows[:count, 3] = (points ** 2).sum(0) + soften
    rows[count:, 3] = 1.0
    return rows


def padded(ref, rows, lanes):
    value = ref[...]
    if value.shape[1] < lanes:
        value = jnp.concatenate([value, jnp.zeros((value.shape[0], lanes - value.shape[1]), value.dtype)], 1)
    if value.shape[0] < rows:
        value = jnp.concatenate([value, jnp.zeros((rows - value.shape[0], lanes), value.dtype)], 0)
    return value


def up_kernel(first_ref, counts_hbm, offsets_hbm, charges_hbm, uc2e_hbm, surface_hbm,
              odd_ref, pair_ref, up_ref, counts_ref, offsets_ref, charges_ref, uc2e_ref, surface_ref, check_ref, sems):
    f32, i32 = jnp.float32, jnp.int32
    copies = []
    for n, (source, target) in enumerate(((counts_hbm, counts_ref), (offsets_hbm, offsets_ref),
                                          (surface_hbm, surface_ref), (charges_hbm, charges_ref),
                                          (uc2e_hbm, uc2e_ref))):
        copies.append(pltpu.make_async_copy(source, target, sems.at[n]))
        copies[n].start()
    probes, points = charges_ref.shape
    local = points // PTS
    lane = lax.broadcasted_iota(i32, (1, PTS), 1)
    sub = lax.broadcasted_iota(i32, (8, PTS), 0)
    first = first_ref[0]
    zero = jnp.zeros((probes, PTS), jnp.bfloat16)
    for copy in copies[:4]:
        copy.wait()
    surface = surface_ref[...]

    for g in range(0, local, 2):
        parts = []
        for h in (g, g + 1):
            at = slice(h * PTS, (h + 1) * PTS)
            parts.append(split(jnp.where(lane < counts_ref[h], charges_ref[:, at], 0.0)))
        both = slice(g * PTS, (g + 2) * PTS)
        tile_hi, tile_lo = split(surface_tile(offsets_ref[:, both] - 0.5, surface))
        left = jnp.concatenate([parts[0][0], zero], 1), jnp.concatenate([zero, parts[1][0]], 1)
        small = jnp.concatenate([parts[0][1], zero], 1), jnp.concatenate([zero, parts[1][1]], 1)
        large = dot_t(jnp.concatenate(left + small, 0), tile_hi)
        fine = dot_t(jnp.concatenate(left, 0), tile_lo)
        value = (large[:2 * probes] + (large[2 * probes:] + fine)) * inv_four_pi
        gap = jnp.zeros((2 * probes, 2 * PTS - value.shape[1]), f32)
        value = jnp.concatenate([value, gap], 1)
        for half in range(2):
            at = slice(half * PTS, (half + 1) * PTS)
            check_ref[half, pl.ds(g, probes, stride=local), :] = value[:probes, at]
            check_ref[half, pl.ds(g + 1, probes, stride=local), :] = value[probes:, at]

    rows = probes * local
    even = lax.rem(lax.div(first, local), 2) == 0
    corner_at = corners(first, local)
    deep = 8 + probes
    for e in range(GHOST):
        ends = e, local - GHOST + e
        for ids, ref, skip in ((ends, odd_ref, 0), (ends[::-1], pair_ref, rows * 5 // 4)):
            h = jnp.where(even, *ids)
            at = pl.multiple_of(h * PTS, PTS)
            corner = [jnp.where(even, corner_at(ids[0], axis), corner_at(ids[1], axis)) for axis in range(3)]
            held = counts_ref[h]
            xyz = jnp.concatenate([offsets_ref[:, pl.ds(at, PTS)], jnp.zeros((5, PTS), f32)], 0)
            move = jnp.where(sub == 0, corner[0], jnp.where(sub == 1, corner[1], jnp.where(sub == 2, corner[2],
                   jnp.where(sub == 3, held.astype(f32), 0.0))))
            ref[skip + e * deep:skip + e * deep + 8] = xyz + move
            ref[skip + e * deep + 8:skip + (e + 1) * deep] = jnp.where(lane < held, charges_ref[:, pl.ds(at, PTS)], 0.0)

    copies[4].wait()
    up = dot_t3(jnp.concatenate([check_ref[0], check_ref[1]], 1), padded(uc2e_ref, 2 * PTS, 2 * PTS))
    rest = rows // 4
    tail = up[:rest, PTS:]
    for k in range(1, 4):
        tail = tail + pltpu.roll(up[k * rest:(k + 1) * rest, PTS:], 32 * k, 1)
    for target in (up_ref, pair_ref):
        target[:rows] = up[:, :PTS]
        target[rows:rows + rest] = tail


def up_call(first, counts, offsets, charges, uc2e):
    local = counts.shape[0]
    probes = charges.shape[0]
    smem = pl.BlockSpec(memory_space=pltpu.SMEM)
    vmem = pl.BlockSpec(memory_space=pltpu.VMEM)
    hbm = pl.BlockSpec(memory_space=pltpu.HBM)
    f32 = jnp.float32
    surface = surface_rows()
    sent = probes * local * 5 // 4
    ghost = GHOST * (8 + probes)
    return pl.pallas_call(
        up_kernel,
        out_shape=(
            jax.ShapeDtypeStruct((ghost, PTS), f32),
            jax.ShapeDtypeStruct((sent + ghost, PTS), f32),
            jax.ShapeDtypeStruct((sent, PTS), f32),
        ),
        in_specs=[smem, hbm, hbm, hbm, hbm, hbm],
        out_specs=(vmem,) * 3,
        scratch_shapes=[
            pltpu.SMEM(counts.shape, jnp.int32),
            pltpu.VMEM(offsets.shape, f32),
            pltpu.VMEM(charges.shape, f32),
            pltpu.VMEM(uc2e.shape, f32),
            pltpu.VMEM(surface.shape, f32),
            pltpu.VMEM((2, probes * local, PTS), f32),
            pltpu.SemaphoreType.DMA((5,)),
        ],
        compiler_params=pltpu.CompilerParams(vmem_limit_bytes=60 << 20),
        cost_estimate=pl.CostEstimate(flops=500_000_000, bytes_accessed=1_500_000, transcendentals=600_000),
        name="upward",
    )(first, counts, offsets, charges, uc2e, jnp.asarray(surface))


def send_order(count):
    half = count // 2
    return [count - 1, *range(half, count - 1), *range(half - 1, 0, -1), 0]


def far_kernel(counts_ref, wanted_ref, tile_hi_ref, tile_lo_ref, near_ref, w_hi_ref, w_lo_ref, twice_ref, dc2e_ref,
               *refs):
    f32, bf16, i32 = jnp.float32, jnp.bfloat16, jnp.int32
    sent = refs[:-7]
    pieces = [sent[i] for i in np.argsort(send_order(len(sent)))]
    out_ref, pick_ref, table_ref, x_hi_ref, x_lo_ref, eq_ref, down_ref = refs[-7:]
    probes, points = out_ref.shape
    local = points // PTS
    bits, cap = wanted_ref.shape
    depth = bits * cap + local
    kinds = w_hi_ref.shape[1] // (PTS + 32)
    twice = twice_ref[...]
    rows = probes * local
    lane = lax.broadcasted_iota(i32, (1, PTS), 1)

    blocks = probes * 5 // 4
    for b in range(bits):
        for c in range(cap):
            pick_ref[pl.ds(b * cap + c, blocks, stride=depth), :] = pieces[b][pl.ds(wanted_ref[b, c], blocks, stride=local), :]
    for n in range(blocks):
        pick_ref[n * depth + bits * cap:(n + 1) * depth, :] = pieces[bits][n * local:(n + 1) * local, :]
    for n in range(blocks):
        hi, lo = split(pick_ref[n * depth:(n + 1) * depth, :])
        table_ref[:depth, n * PTS:(n + 1) * PTS] = hi
        table_ref[depth:, n * PTS:(n + 1) * PTS] = lo

    group = lane // 32
    quarter = probes // 4
    def spread(part, q):
        hi, lo = split(part)
        for t in range(kinds):
            x_hi_ref[q * local:(q + 1) * local, t * PTS:(t + 1) * PTS] = hi[t * local:(t + 1) * local]
            x_lo_ref[q * local:(q + 1) * local, t * PTS:(t + 1) * PTS] = lo[t * local:(t + 1) * local]

    def spread_rest(part, q):
        for t in range(0, kinds, 4):
            kinds4 = [part[(t + i) * local:(t + i + 1) * local] for i in range(4)]

            def mix(pick):
                value = pick(3)
                for i in range(3):
                    value = jnp.where(group == i, pick(i), value)
                return value

            moved = []
            for shift in range(4):
                value = mix(lambda k: kinds4[(k + shift) % 4])
                moved.append(pltpu.roll(value, 32 * shift, 1) if shift else value)
            at = kinds * PTS + t * 32
            for k in range(4):
                to = (q + quarter * k) * local
                value = mix(lambda i: moved[(i - k) % 4])
                x_hi_ref[to:to + local, at:at + PTS], x_lo_ref[to:to + local, at:at + PTS] = split(value)

    for n in range(0, probes, 2):
        both = dot(twice, table_ref[:, n * PTS:(n + 2) * PTS])
        spread(both[:, :PTS], n)
        spread(both[:, PTS:], n + 1)

    def down_part(at):
        x_hi, x_lo, w_hi, w_lo = x_hi_ref[:, at], x_lo_ref[:, at], w_hi_ref[:, at], w_lo_ref[:, at]
        return dot_t(jnp.concatenate([x_hi, x_hi, x_lo], 1), jnp.concatenate([w_hi, w_lo, w_hi], 1))

    for q in range(quarter):
        spread_rest(dot(twice, table_ref[:, (probes + q) * PTS:(probes + q + 1) * PTS]), q)

    def add_part(i, _):
        down_ref[...] += down_part(pl.ds(pl.multiple_of(i * cut, PTS), cut))
        return 0

    cut = kinds * (PTS + 32) // 2
    down_ref[...] = jnp.zeros_like(down_ref)
    lax.fori_loop(0, 2, add_part, 0)
    down = down_ref[...]
    equivs = dot_t3(down, padded(dc2e_ref, 2 * PTS, down.shape[1]))
    eq_ref[0], eq_ref[1] = equivs[:, :PTS], equivs[:, PTS:]

    reach = tile_hi_ref.shape[0]
    for g in range(0, local, 2):
        at = slice(g * PTS, (g + 2) * PTS)
        tile_hi, tile_lo = tile_hi_ref[:, at], tile_lo_ref[:, at]
        parts = []
        for h in (g, g + 1):
            value = jnp.concatenate([eq_ref[half, pl.ds(h, probes, stride=local), :] for half in range(2)], 1)[:, :reach]
            parts.append(split(value))
        left = parts[0][0], parts[1][0]
        large = dot(jnp.concatenate(left + (parts[0][1], parts[1][1]), 0), tile_hi)
        value = large[:2 * probes] + (large[2 * probes:] + dot(jnp.concatenate(left, 0), tile_lo))
        for i in range(2):
            h = g + i
            to = slice(h * PTS, (h + 1) * PTS)
            part = value[i * probes:(i + 1) * probes, i * PTS:(i + 1) * PTS] * inv_four_pi
            out_ref[:, to] = jnp.where(lane < counts_ref[h], near_ref[:, to] + part, 0.0)


def far_call(counts, wanted, tiles, near, w_hi, w_lo, twice, dc2e, pieces):
    local = counts.shape[0]
    probes, points = near.shape
    kinds = w_hi.shape[1] // (PTS + 32)
    smem = pl.BlockSpec(memory_space=pltpu.SMEM)
    vmem = pl.BlockSpec(memory_space=pltpu.VMEM)
    f32, bf16 = jnp.float32, jnp.bfloat16
    rows = probes * local
    wide = kinds * (PTS + 32)
    depth = wanted.shape[0] * wanted.shape[1] + local
    return pl.pallas_call(
        far_kernel,
        out_shape=jax.ShapeDtypeStruct((probes, points), f32),
        in_specs=[smem, smem] + [vmem] * (7 + len(pieces)),
        out_specs=vmem,
        scratch_shapes=[
            pltpu.VMEM((probes * 5 // 4 * depth, PTS), f32),
            pltpu.VMEM((2 * depth, probes * 5 // 4 * PTS), bf16),
            pltpu.VMEM((rows, wide), bf16),
            pltpu.VMEM((rows, wide), bf16),
            pltpu.VMEM((2, rows, PTS), f32),
            pltpu.VMEM((rows, w_hi.shape[0]), f32),
        ],
        compiler_params=pltpu.CompilerParams(vmem_limit_bytes=32 << 20),
        cost_estimate=pl.CostEstimate(flops=4_000_000_000, bytes_accessed=4_000_000, transcendentals=600_000),
        name="far",
    )(counts, wanted, *tiles, near, w_hi, w_lo, twice, dc2e, *(pieces[i] for i in send_order(len(pieces))))


def shards(offsets, charges, counts, u_list, v_src, v_type, wanted, m2l, uc2e, dc2e):
    local_leaves = counts.shape[0]
    first = (lax.axis_index("cube") * local_leaves).astype(jnp.int32).reshape(1)
    odd, pair, up = up_call(first, counts, offsets, charges, uc2e)
    count = lax.axis_size("cube")
    odd = lax.ppermute(odd, "cube", [(i, i + 1 if i % 2 else i - 1) for i in range(1, count - 1)])
    pieces = [from_partner(up, "cube", bit) for bit in range(count.bit_length() - 2, 0, -1)]
    pair = from_partner(pair, "cube", 0)
    pieces = [pair] + pieces[::-1] + [up]
    depth = wanted.shape[1] * wanted.shape[2] + counts.shape[0]
    near, w_hi, w_lo, twice, *tiles = near_call(first, counts, offsets, charges, pair, odd, u_list, m2l, v_src, v_type, depth)
    return far_call(counts, wanted[0], tiles, near, w_hi, w_lo, twice, dc2e, pieces)


def solution(mesh):
    in_specs = (
        P(None, "cube"),
        P(None, "cube"),
        P("cube"),
        P("cube", None),
        P("cube", None),
        P("cube", None),
        P("cube", None, None),
        P(),
        P(),
        P(),
    )
    out_specs = P(None, "cube")
    return jax.shard_map(shards, mesh=mesh, in_specs=in_specs, out_specs=out_specs, check_vma=False)
```
